768 devices in a mesh: seq: 96 (over x, z, core), head: 8 (over y).
Axes of the slice: x: 4, y: 8, z: 12, core: 2. Of those that a mesh axis runs over, the one named last changes fastest.
Arguments:
- queries: bfloat16 [12288, 4096], P('seq', 'head'), may hold values from -6 to 6
- keys: bfloat16 [12288, 4096], P('seq', 'head'), may hold values from -6 to 6
- values: bfloat16 [12288, 4096], P('seq', 'head'), may hold values from -3 to 3
- decay_codes: int32 [12288, 32], P('seq', 'head'), may hold values from 0 to 2048
- out_weight: bfloat16 [4096, 3072], P('head'), may hold values from -0.09375 to 0.09375
- out_grad: bfloat16 [12288, 3072], P('seq', 'head'), may hold values from -6 to 6
Outputs:
- mixed: bfloat16 [12288, 3072], P('seq', 'head')
- query_gradient: bfloat16 [12288, 4096], P('seq', 'head')
- key_grad: bfloat16 [12288, 4096], P('seq', 'head')
- value_gradient: bfloat16 [12288, 4096], P('seq', 'head')
The draws below stay inside these ranges and needn't reach their ends.
All inputs are finite; a program needn't handle non-finite values.
Results may differ from the reference program's by a relative error of at most 0.014.
Values may be sent and summed in bfloat16 or wider, within the bound.
A program may use at most 128 MiB of HBM per device.

```python
import jax
import jax.numpy as jnp
from jax import lax

D = 3072
HEADS = 32
HEAD_DIM = 128
TOK_DEV = 128
TOKENS = 12288


def draw_decay_codes(key, part):
    keys_all = jax.random.split(key, 5)
    order = jax.random.permutation(keys_all[0], HEADS)
    slow_heads = order < HEADS // 2
    quick_decay_labels = jax.random.randint(keys_all[1], (TOKENS, HEADS), 100, 134)
    block_place = jnp.arange(TOKENS) // TOK_DEV
    head_offset = jax.random.randint(keys_all[4], (HEADS,), 0, 8)
    quick_block = (block_place[:, None] + head_offset[None, :]) % 8 == 0
    quick_here = jnp.logical_and(quick_block, jnp.logical_not(slow_heads)[None, :])
    baseline_decay_labels = jnp.where(quick_here, quick_decay_labels, 0)
    segment_places = jax.random.randint(keys_all[2], (3, HEADS), 0, TOKENS)
    nesting_level = jax.random.randint(keys_all[3], (3, HEADS), 820, 2049)
    nesting_level = nesting_level.at[0, 0].set(2048)
    token_places = jnp.arange(TOKENS)[:, None, None]
    segment_span = jnp.max(jnp.where(token_places == segment_places[None], nesting_level[None], 0), axis=1)
    return jnp.maximum(baseline_decay_labels, segment_span).astype(jnp.int32)


def level_of(own_key, extent, cuts, least, high):
    gain, own = 1.0, jax.random.fold_in(own_key, 6)
    for position, parts in cuts:
        heights = jnp.exp(jax.random.uniform(jax.random.fold_in(own, position), (parts,), jnp.float32, least / len(cuts), high / len(cuts)))
        gain = gain * jnp.repeat(heights, extent[position] // parts).reshape([-1 if axis == position else 1 for axis in range(len(extent))])
    return gain


def centred(key, extent, width, reach, pieces=(), dtype=jnp.bfloat16):
    gain = level_of(key, extent, pieces, -0.22, 0.18) if pieces else 1.0
    entries = jax.random.normal(key, extent, jnp.float32) * width * gain
    return jnp.minimum(jnp.maximum(entries, -reach), reach).astype(dtype)


def setup_inputs(seed: int = 0) -> dict:
    streams_of = jax.random.split(jax.random.key(seed), 7)
    return {
        "queries": centred(streams_of[0], (TOKENS, HEADS * HEAD_DIM), 1.0, 6.0, ((0, 96), (1, 8))),
        "keys": centred(streams_of[1], (TOKENS, HEADS * HEAD_DIM), 1.0, 6.0, ((0, 96), (1, 8))),
        "values": centred(streams_of[2], (TOKENS, HEADS * HEAD_DIM), 0.5, 3.0, ((0, 96), (1, 8))),
        "decay_codes": draw_decay_codes(jax.random.fold_in(streams_of[6], 71), 0),
        "out_weight": centred(streams_of[4], (HEADS * HEAD_DIM, D), (HEADS * HEAD_DIM) ** -0.5, 0.09375, ((0, 8),)),
        "out_grad": centred(streams_of[5], (TOKENS, D), 1.0, 6.0, ((0, 96), (1, 8))),
    }


def block_mask(cum_log):
    block_len = cum_log.shape[0]
    log_gap = cum_log.T[:, :, None] - cum_log.T[:, None, :]
    lower_part = (jnp.arange(block_len)[:, None] >= jnp.arange(block_len)[None, :])[None]
    return jnp.where(lower_part, jnp.exp(jnp.where(lower_part, log_gap, 0.0)), 0.0)


def factors(code_block):
    cum_log = jnp.cumsum(jnp.log(1.0 - code_block.astype(jnp.float32) / 4096.0), axis=0)
    rise_decay = jnp.exp(cum_log)
    fall_decay = jnp.exp(cum_log[-1][None, :] - cum_log)
    total_decay = jnp.exp(cum_log[-1])
    return block_mask(cum_log), rise_decay, fall_decay, total_decay


def local_terms(query_h, key_h, value_h, grad_h, code_block):
    att_scale = 1.0 / HEAD_DIM
    decay_mask, rise_decay, fall_decay, total_decay = factors(code_block)
    query_f = query_h.astype(jnp.float32)
    key_f = key_h.astype(jnp.float32)
    value_f = value_h.astype(jnp.float32)
    grad_f = grad_h.astype(jnp.float32)
    scores = jnp.einsum('she,the->hst', query_f, key_f)
    attn = (att_scale * scores * decay_mask).astype(jnp.bfloat16)
    pscores = jnp.einsum('she,the->hst', grad_f, value_f)
    pmat = (att_scale * pscores * decay_mask).astype(jnp.bfloat16)
    q_rise = (att_scale * rise_decay[:, :, None] * query_f).astype(jnp.bfloat16)
    g_rise = (att_scale * rise_decay[:, :, None] * grad_f).astype(jnp.bfloat16)
    k_fall = (fall_decay[:, :, None] * key_f).astype(jnp.bfloat16)
    v_fall = (fall_decay[:, :, None] * value_f).astype(jnp.bfloat16)
    return attn, pmat, q_rise, g_rise, k_fall, v_fall, total_decay


def reference(queries, keys, values, decay_codes, out_weight, out_grad):
    blocks = TOKENS // TOK_DEV
    grad_out = jnp.dot(out_grad, out_weight.T, preferred_element_type=jnp.float32).astype(jnp.bfloat16)

    def to_heads(array):
        return array.reshape(blocks, TOK_DEV, HEADS, HEAD_DIM)

    inputs = (to_heads(queries), to_heads(keys), to_heads(values), to_heads(grad_out),
              decay_codes.reshape(blocks, TOK_DEV, HEADS))

    def forward(state_in, block_item):
        query_h, key_h, value_h, grad_h, code_block = block_item
        attn, pmat, q_rise, g_rise, k_fall, v_fall, total_decay = local_terms(query_h, key_h, value_h, grad_h, code_block)
        state_b = state_in.astype(jnp.bfloat16).astype(jnp.float32)
        attn_out = jnp.einsum('hst,the->she', attn.astype(jnp.float32), value_h.astype(jnp.float32))
        attn_out = attn_out + jnp.einsum('shd,hde->she', q_rise.astype(jnp.float32), state_b)
        query_gradient = jnp.einsum('hst,thd->shd', pmat.astype(jnp.float32), key_h.astype(jnp.float32))
        query_gradient = query_gradient + jnp.einsum('she,hde->shd', g_rise.astype(jnp.float32), state_b)
        summary = jnp.einsum('thd,the->hde', k_fall.astype(jnp.float32), value_h.astype(jnp.float32))
        state_next = total_decay[:, None, None] * state_in + summary
        return state_next, (attn_out.astype(jnp.bfloat16), query_gradient.astype(jnp.bfloat16))

    def backward(carried, block_item):
        query_h, key_h, value_h, grad_h, code_block = block_item
        attn, pmat, q_rise, g_rise, k_fall, v_fall, total_decay = local_terms(query_h, key_h, value_h, grad_h, code_block)
        carry_b = carried.astype(jnp.bfloat16).astype(jnp.float32)
        key_grad = jnp.einsum('hst,shd->thd', pmat.astype(jnp.float32), query_h.astype(jnp.float32))
        key_grad = key_grad + jnp.einsum('the,hde->thd', v_fall.astype(jnp.float32), carry_b)
        value_gradient = jnp.einsum('hst,she->the', attn.astype(jnp.float32), grad_h.astype(jnp.float32))
        value_gradient = value_gradient + jnp.einsum('thd,hde->the', k_fall.astype(jnp.float32), carry_b)
        summary = jnp.einsum('shd,she->hde', q_rise.astype(jnp.float32), grad_h.astype(jnp.float32))
        carry_next = total_decay[:, None, None] * carried + summary
        return carry_next, (key_grad.astype(jnp.bfloat16), value_gradient.astype(jnp.bfloat16))

    zero_state = jnp.zeros((HEADS, HEAD_DIM, HEAD_DIM), jnp.float32)
    state_end, (attn_out, query_gradient) = lax.scan(forward, zero_state, inputs)
    carry_end, (key_grad, value_gradient) = lax.scan(backward, zero_state, inputs, reverse=True)
    width_all = HEADS * HEAD_DIM
    attn_flat = attn_out.reshape(TOKENS, width_all)
    mixed = jnp.dot(attn_flat, out_weight, preferred_element_type=jnp.float32).astype(jnp.bfloat16)
    return (mixed, query_gradient.reshape(TOKENS, width_all), key_grad.reshape(TOKENS, width_all),
            value_gradient.reshape(TOKENS, width_all))
```

```python
import jax
import jax.numpy as jnp
from jax import lax
from jax.experimental import pallas as pl
from jax.experimental.pallas import tpu as pltpu
from jax.sharding import PartitionSpec as P

MESH = pl.DeviceIdType.MESH
BF16 = jnp.bfloat16
F32 = jnp.float32
NX, NZ, NC, NY = 4, 12, 2, 8
ZG = 4
GROUPS = NZ // ZG
MEMBERS = ZG * NC
TOK = 128
HW = 128
NH = 4
COLS = 384
HALF = HW // 2
PIECE = HALF + 16
SCALE = 1.0 / HW


def nn(a, b):
    return lax.dot_general(a, b, (((1,), (0,)), ((), ())), preferred_element_type=F32)


def nt(a, b):
    return lax.dot_general(a, b, (((1,), (1,)), ((), ())), preferred_element_type=F32)


def tn(a, b):
    return lax.dot_general(a, b, (((0,), (0,)), ((), ())), preferred_element_type=F32)


def log_tile(log_total):
    high = log_total.astype(BF16)
    rest = log_total - high.astype(F32)
    mid = rest.astype(BF16)
    low = (rest - mid.astype(F32)).astype(BF16)
    row = lax.broadcasted_iota(jnp.int32, (16, HW), 0)
    parts = [jnp.broadcast_to(part.astype(F32), (16, HW)) for part in (high, mid, low)]
    tile = jnp.where(row == 0, parts[0], jnp.where(row == 1, parts[1], jnp.where(row == 2, parts[2], 0.0)))
    return tile.astype(BF16)


def log_of(piece):
    return jnp.sum(piece[HALF:PIECE].astype(F32), axis=0, keepdims=True)


class Scan:
    def __init__(self, place, reverse, refs):
        self.x, self.z, self.c, self.y = place
        self.reverse = reverse
        (self.psend, self.precv, self.gsend, self.zrecv, self.xsend, self.xrecv, self.bsend, self.brecv,
         self.ps, self.pr, self.zs, self.zr, self.xs, self.xr, self.bs, self.br) = refs
        self.group = self.z // ZG
        self.me = lax.rem(self.z, ZG) * NC + self.c
        self.sent = []

    def device(self, x, z, c):
        return {"seq": x * (NZ * NC) + z * NC + c, "head": self.y}

    def member(self, m):
        return self.device(self.x, self.group * ZG + m // NC, lax.rem(m, NC))

    def copy(self, src, dst, ss, rs, where):
        return pltpu.make_async_remote_copy(src, dst, ss, rs, device_id=where, device_id_type=MESH)

    def put(self, head, summary, log_total):
        tile = log_tile(log_total)
        data = summary.astype(BF16)
        for half in range(2):
            self.psend[2 * head + half, 0:HALF, :] = data[half * HALF:(half + 1) * HALF]
            self.psend[2 * head + half, HALF:PIECE, :] = tile

    def start_pieces(self):
        for k in range(1, MEMBERS):
            to = lax.rem(self.me + k, MEMBERS)
            copy = self.copy(self.psend.at[to], self.precv.at[self.me], self.ps.at[k], self.pr.at[k], self.member(to))
            copy.start()
            self.sent.append(copy)
        self.precv[self.me] = self.psend[self.me]

    def wait_pieces(self):
        for k in range(1, MEMBERS):
            self.sent[k - 1].wait_recv()

    def order(self, count):
        return reversed(range(count)) if self.reverse else range(count)

    def group_total(self):
        total = jnp.zeros((HALF, HW), F32)
        log_total = jnp.zeros((1, HW), F32)
        for m in self.order(MEMBERS):
            piece = self.precv[m]
            log_m = log_of(piece)
            total = jnp.exp(log_m) * total + piece[0:HALF].astype(F32)
            log_total = log_total + log_m
        self.gsend[0:HALF, :] = total.astype(BF16)
        self.gsend[HALF:PIECE, :] = log_tile(log_total)

    def start_groups(self):
        self.zcopies = []
        for k in range(1, GROUPS):
            to = lax.rem(self.group + k, GROUPS)
            copy = self.copy(self.gsend, self.zrecv.at[self.group], self.zs.at[k], self.zr.at[k],
                             self.device(self.x, to * ZG + lax.rem(self.z, ZG), self.c))
            copy.start()
            self.zcopies.append(copy)
        self.zrecv[self.group] = self.gsend[...]

    def prefix(self, recv, count, place):
        before = jnp.zeros((HALF, HW), F32)
        log_before = jnp.zeros((1, HW), F32)
        total = jnp.zeros((HALF, HW), F32)
        log_total = jnp.zeros((1, HW), F32)
        for m in self.order(count):
            before = jnp.where(place == m, total, before)
            log_before = jnp.where(place == m, log_total, log_before)
            piece = recv[m]
            log_m = log_of(piece)
            total = jnp.exp(log_m) * total + piece[0:HALF].astype(F32)
            log_total = log_total + log_m
        return before, log_before, total, log_total

    def wait_groups(self):
        for copy in self.zcopies:
            copy.wait_recv()

    def start_planes(self):
        self.before, self.log_before, total, log_total = self.prefix(self.zrecv, GROUPS, self.group)
        self.xsend[0:HALF, :] = total.astype(BF16)
        self.xsend[HALF:PIECE, :] = log_tile(log_total)
        self.xcopies = []
        for k in range(1, NX):
            to = lax.rem(self.x + k, NX)
            copy = self.copy(self.xsend, self.xrecv.at[self.x], self.xs.at[k], self.xr.at[k],
                             self.device(to, self.z, self.c))
            copy.start()
            self.xcopies.append(copy)
        self.xrecv[self.x] = self.xsend[...]

    def wait_planes(self):
        for copy in self.xcopies:
            copy.wait_recv()

    def start_back(self):
        entering, _, _, _ = self.prefix(self.xrecv, NX, self.x)
        state = jnp.exp(self.log_before) * entering + self.before
        for m in self.order(MEMBERS):
            self.bsend[m] = state.astype(BF16)
            piece = self.precv[m]
            state = jnp.exp(log_of(piece)) * state + piece[0:HALF].astype(F32)
        self.bcopies = []
        rows = pl.ds(pl.multiple_of(self.me * HALF, HALF), HALF)
        for k in range(1, MEMBERS):
            to = lax.rem(self.me + k, MEMBERS)
            copy = self.copy(self.bsend.at[to], self.brecv.at[rows], self.bs.at[k], self.br.at[k], self.member(to))
            copy.start()
            self.bcopies.append(copy)
        self.brecv[rows, :] = self.bsend[self.me]

    def wait_back(self):
        for copy in self.bcopies:
            copy.wait_recv()

    def finish(self):
        for copy in self.sent + self.zcopies + self.xcopies + self.bcopies:
            copy.wait_send()


SCAN_BUFFERS = [
    pltpu.VMEM((MEMBERS, PIECE, HW), BF16),
    pltpu.VMEM((MEMBERS, PIECE, HW), BF16),
    pltpu.VMEM((PIECE, HW), BF16),
    pltpu.VMEM((GROUPS, PIECE, HW), BF16),
    pltpu.VMEM((PIECE, HW), BF16),
    pltpu.VMEM((NX, PIECE, HW), BF16),
    pltpu.VMEM((MEMBERS, HALF, HW), BF16),
    pltpu.VMEM((NH * HW, HW), BF16),
    pltpu.SemaphoreType.DMA((MEMBERS,)),
    pltpu.SemaphoreType.DMA((MEMBERS,)),
    pltpu.SemaphoreType.DMA((GROUPS,)),
    pltpu.SemaphoreType.DMA((GROUPS,)),
    pltpu.SemaphoreType.DMA((NX,)),
    pltpu.SemaphoreType.DMA((NX,)),
    pltpu.SemaphoreType.DMA((MEMBERS,)),
    pltpu.SemaphoreType.DMA((MEMBERS,)),
]
NB = len(SCAN_BUFFERS)


def kernel(q_ref, k_ref, v_ref, codes_ref, w_hbm, og_ref, mixed_ref, qg_ref, kg_ref, vg_ref, *scratch):
    fwd_refs, bwd_refs, rest = scratch[:NB], scratch[NB:2 * NB], scratch[2 * NB:]
    (w_ref, w_sem, ag, ag_ss, ag_rs, rs_send, rs_recv, rs_ss, rs_rs,
     attn_s, kfall_s, qrise_s, grad_s, out_s, qg_s, kg_s, vg_s, rise_s, fall_s) = rest
    seq, y = lax.axis_index("seq"), lax.axis_index("head")
    x, z, c = seq // (NZ * NC), lax.rem(seq, NZ * NC) // NC, lax.rem(seq, NC)
    place = (x, z, c, y)
    fwd, bwd = Scan(place, False, fwd_refs), Scan(place, True, bwd_refs)

    w_copy = pltpu.make_async_copy(w_hbm, w_ref, w_sem)
    w_copy.start()

    def row(offset):
        return {"seq": seq, "head": lax.rem(y + NY + offset, NY)}

    barrier = pltpu.get_barrier_semaphore()
    greeted = [fwd.member(lax.rem(fwd.me + k, MEMBERS)) for k in range(1, MEMBERS)]
    greeted += [fwd.device(x, lax.rem(z + k * ZG, NZ), c) for k in range(1, GROUPS)]
    greeted += [fwd.device(lax.rem(x + k, NX), z, c) for k in range(1, NX)]
    greeted += [row(k) for k in (1, -1, 2, -2)]
    for where in greeted:
        pl.semaphore_signal(barrier, inc=1, device_id=where, device_id_type=MESH)

    rate = 1.0 - codes_ref[...].astype(F32) * (1.0 / 4096.0)
    logs = jnp.log(rate)
    ri = lax.broadcasted_iota(jnp.int32, (TOK, TOK), 0)
    ci = lax.broadcasted_iota(jnp.int32, (TOK, TOK), 1)
    lower = ri >= ci
    log_pad = jnp.zeros((TOK, TOK), F32)
    for h in range(NH):
        log_pad = jnp.where(ci == h, logs[:, h:h + 1], log_pad)
    cum = lax.dot_general(lower.astype(F32), log_pad, (((1,), (0,)), ((), ())),
                          precision=lax.Precision.HIGHEST, preferred_element_type=F32)
    cum_t = cum.T
    heads = [slice(h * HW, (h + 1) * HW) for h in range(NH)]
    for h in range(NH):
        column = jnp.broadcast_to(cum[:, h:h + 1], (TOK, HW))
        last = column[TOK - 1:TOK]
        fall = jnp.exp(last - column)
        fall_s[h] = fall
        rise_s[h] = jnp.exp(column) * SCALE
        k_fall = (fall * k_ref[:, heads[h]].astype(F32)).astype(BF16)
        kfall_s[:, heads[h]] = k_fall
        fwd.put(h, tn(k_fall, v_ref[:, heads[h]]), last)

    pl.semaphore_wait(barrier, len(greeted))
    fwd.start_pieces()
    ag_copies = {}
    for i, k in enumerate((2, -2, 1, -1)):
        ag_copies[k] = pltpu.make_async_remote_copy(
            og_ref, ag.at[y], ag_ss.at[i], ag_rs.at[i], device_id=row(k), device_id_type=MESH)
        ag_copies[k].start()

    masks = []
    for h in range(NH):
        column = jnp.broadcast_to(cum[:, h:h + 1], (TOK, TOK))
        gap = column - cum_t[h:h + 1, :]
        mask = jnp.where(lower, jnp.exp(jnp.where(lower, gap, 0.0)), 0.0) * SCALE
        masks.append(mask)
        q_h, k_h, v_h = q_ref[:, heads[h]], k_ref[:, heads[h]], v_ref[:, heads[h]]
        attn = (nt(q_h, k_h) * mask).astype(BF16)
        attn_s[h] = attn
        qrise_s[:, heads[h]] = (rise_s[h] * q_h.astype(F32)).astype(BF16)
        out_s[:, heads[h]] = nn(attn, v_h)

    w_copy.wait()

    def w_cols(owner):
        return w_ref[:, pl.ds(pl.multiple_of(owner * COLS, 128), COLS)]

    grad_s[...] = nt(og_ref[...], w_cols(y))

    def add_grad(offset):
        owner = lax.rem(y + NY + offset, NY)
        grad_s[...] += nt(ag[owner], w_cols(owner))

    for sign, i, rows in ((1, 4, slice(0, HALF)), (-1, 6, slice(HALF, TOK))):
        ag_copies[2 * sign].wait_recv()
        owner = lax.rem(y + NY - 2 * sign, NY)
        ag_copies[4 * sign] = pltpu.make_async_remote_copy(
            ag.at[owner, rows], ag.at[owner, rows], ag_ss.at[i + 1], ag_rs.at[i + 1],
            device_id=row(2 * sign), device_id_type=MESH)
        ag_copies[4 * sign].start()
        ag_copies[3 * sign] = pltpu.make_async_remote_copy(
            ag.at[owner], ag.at[owner], ag_ss.at[i], ag_rs.at[i], device_id=row(sign), device_id_type=MESH)
        ag_copies[3 * sign].start()
    fwd.wait_pieces()
    fwd.group_total()
    fwd.start_groups()
    add_grad(2)
    add_grad(-2)
    for sign in (1, -1):
        ag_copies[sign].wait_recv()
        add_grad(-sign)
    for sign in (1, -1):
        ag_copies[3 * sign].wait_recv()
        add_grad(-3 * sign)
    for sign in (1, -1):
        ag_copies[4 * sign].wait_recv()
    add_grad(4)
    fwd.wait_groups()
    fwd.start_planes()
    for h in range(NH):
        last = jnp.broadcast_to(cum[TOK - 1:TOK, h:h + 1], (1, HW))
        bwd.put(h, tn(qrise_s[:, heads[h]], grad_s[:, heads[h]].astype(BF16)), last)
    bwd.start_pieces()
    fwd.wait_planes()
    fwd.start_back()

    for h in range(NH):
        g_h = grad_s[:, heads[h]].astype(BF16)
        q_h, k_h, v_h = q_ref[:, heads[h]], k_ref[:, heads[h]], v_ref[:, heads[h]]
        pmat = (nt(g_h, v_h) * masks[h]).astype(BF16)
        qg_s[:, heads[h]] = nn(pmat, k_h)
        kg_s[:, heads[h]] = tn(pmat, q_h)
        vg_s[:, heads[h]] = tn(attn_s[h], g_h)

    bwd.wait_pieces()
    bwd.group_total()
    bwd.start_groups()

    fwd.wait_back()
    for h in range(NH):
        out_s[:, heads[h]] += nn(qrise_s[:, heads[h]], fwd.brecv[heads[h], :])
    attn_out = out_s[...].astype(BF16)

    def part(offset):
        return nn(attn_out, w_cols(lax.rem(y + NY + offset, NY)))

    rs = {}

    def send(key, i, src, dst, where):
        rs[key] = pltpu.make_async_remote_copy(
            src, dst, rs_ss.at[i], rs_rs.at[i], device_id=where, device_id_type=MESH)
        rs[key].start()

    rs_send[0] = part(4).astype(BF16)
    send(4, 0, rs_send.at[0, 0:HALF], rs_recv.at[0, 0:HALF], row(2))
    send(-4, 1, rs_send.at[0, HALF:TOK], rs_recv.at[0, HALF:TOK], row(-2))
    for slot, k in ((1, 3), (2, -3)):
        rs_send[slot] = part(k).astype(BF16)
        send(k, 1 + slot, rs_send.at[slot], rs_recv.at[slot], row(1 if k > 0 else -1))
    for slot, k in ((3, 1), (4, -1)):
        rs_send[slot] = part(k).astype(BF16)
        send(k, 1 + slot, rs_send.at[slot], rs_recv.at[slot], row(k))
    onward = {1: part(2), -1: part(-2)}
    own = part(0)

    bwd.wait_groups()
    bwd.start_planes()

    for slot, sign, rows in ((5, 1, slice(0, HALF)), (6, -1, slice(HALF, TOK))):
        rs[3 * sign].wait_recv()
        rs[4 * sign].wait_recv()
        total = onward[sign] + rs_recv[1 if sign > 0 else 2].astype(F32)
        near = rs_recv[0, rows].astype(F32)
        if sign > 0:
            rs_send[slot, 0:HALF] = (total[0:HALF] + near).astype(BF16)
            rs_send[slot, HALF:TOK] = total[HALF:TOK].astype(BF16)
        else:
            rs_send[slot, 0:HALF] = total[0:HALF].astype(BF16)
            rs_send[slot, HALF:TOK] = (total[HALF:TOK] + near).astype(BF16)
        send(2 * sign, 1 + slot, rs_send.at[slot], rs_recv.at[slot], row(2 * sign))

    bwd.wait_planes()
    bwd.start_back()

    for h in range(NH):
        g_rise = (rise_s[h] * grad_s[:, heads[h]].astype(BF16).astype(F32)).astype(BF16)
        qg_ref[:, heads[h]] = (qg_s[:, heads[h]] + nt(g_rise, fwd.brecv[heads[h], :])).astype(BF16)

    for key in (1, -1, 2, -2):
        rs[key].wait_recv()
    total = own
    for slot in (3, 4, 5, 6):
        total = total + rs_recv[slot].astype(F32)
    mixed_ref[...] = total.astype(BF16)

    bwd.wait_back()
    for h in range(NH):
        carry = bwd.brecv[heads[h], :]
        v_fall = (fall_s[h] * v_ref[:, heads[h]].astype(F32)).astype(BF16)
        kg_ref[:, heads[h]] = (kg_s[:, heads[h]] + nt(v_fall, carry)).astype(BF16)
        vg_ref[:, heads[h]] = (vg_s[:, heads[h]] + nn(kfall_s[:, heads[h]], carry)).astype(BF16)

    fwd.finish()
    bwd.finish()
    for copy in list(ag_copies.values()) + list(rs.values()):
        copy.wait_send()


def local(queries, keys, values, decay_codes, out_weight, out_grad):
    vmem = pl.BlockSpec(memory_space=pltpu.VMEM)
    wide = NH * HW
    return pl.pallas_call(
        kernel,
        out_shape=(
            jax.ShapeDtypeStruct((TOK, COLS), BF16),
            jax.ShapeDtypeStruct((TOK, wide), BF16),
            jax.ShapeDtypeStruct((TOK, wide), BF16),
            jax.ShapeDtypeStruct((TOK, wide), BF16),
        ),
        in_specs=[vmem, vmem, vmem, vmem, pl.BlockSpec(memory_space=pl.ANY), vmem],
        out_specs=(vmem,) * 4,
        scratch_shapes=SCAN_BUFFERS + SCAN_BUFFERS + [
            pltpu.VMEM(out_weight.shape, BF16),
            pltpu.SemaphoreType.DMA,
            pltpu.VMEM((NY, TOK, COLS), BF16),
            pltpu.SemaphoreType.DMA((8,)),
            pltpu.SemaphoreType.DMA((8,)),
            pltpu.VMEM((7, TOK, COLS), BF16),
            pltpu.VMEM((7, TOK, COLS), BF16),
            pltpu.SemaphoreType.DMA((8,)),
            pltpu.SemaphoreType.DMA((8,)),
            pltpu.VMEM((NH, TOK, TOK), BF16),
            pltpu.VMEM((TOK, wide), BF16),
            pltpu.VMEM((TOK, wide), BF16),
            pltpu.VMEM((TOK, wide), F32),
            pltpu.VMEM((TOK, wide), F32),
            pltpu.VMEM((TOK, wide), F32),
            pltpu.VMEM((TOK, wide), F32),
            pltpu.VMEM((TOK, wide), F32),
            pltpu.VMEM((NH, TOK, HW), F32),
            pltpu.VMEM((NH, TOK, HW), F32),
        ],
        name="linear_attention",
        compiler_params=pltpu.CompilerParams(
            collective_id=0, has_side_effects=True, vmem_limit_bytes=40 * 1024 * 1024
        ),
    )(queries, keys, values, decay_codes, out_weight, out_grad)


def solution(mesh):
    placed = (
        P("seq", "head"),
        P("seq", "head"),
        P("seq", "head"),
        P("seq", "head"),
        P("head", None),
        P("seq", "head"),
    )
    return jax.shard_map(
        local,
        mesh=mesh,
        in_specs=placed,
        out_specs=(P("seq", "head"), P("seq", "head"), P("seq", "head"), P("seq", "head")),
        check_vma=False,
    )
```

```python
import contextlib

import jax
import jax.numpy as jnp
from jax import lax
from jax.experimental import pallas as pl
from jax.experimental.pallas import tpu as pltpu
from jax.sharding import PartitionSpec as P

MESH = pl.DeviceIdType.MESH
BF16 = jnp.bfloat16
F32 = jnp.float32
NX, NZ, NC, NY = 4, 12, 2, 8
ZG = 4
GROUPS = NZ // ZG
MEMBERS = ZG * NC
TOK = 128
HW = 128
NH = 4
COLS = 384
HALF = HW // 2
PIECE = HALF + 16
SCALE = 1.0 / HW
TRACE = False


def scope(name):
    return jax.named_scope(name) if TRACE else contextlib.nullcontext()


def nn(a, b):
    return lax.dot_general(a, b, (((1,), (0,)), ((), ())), preferred_element_type=F32)


def nt(a, b):
    return lax.dot_general(a, b, (((1,), (1,)), ((), ())), preferred_element_type=F32)


def tn(a, b):
    return lax.dot_general(a, b, (((0,), (0,)), ((), ())), preferred_element_type=F32)


def log_tile(log_total):
    high = log_total.astype(BF16)
    rest = log_total - high.astype(F32)
    mid = rest.astype(BF16)
    low = (rest - mid.astype(F32)).astype(BF16)
    row = lax.broadcasted_iota(jnp.int32, (16, HW), 0)
    parts = [jnp.broadcast_to(part.astype(F32), (16, HW)) for part in (high, mid, low)]
    tile = jnp.where(row == 0, parts[0], jnp.where(row == 1, parts[1], jnp.where(row == 2, parts[2], 0.0)))
    return tile.astype(BF16)


def log_of(piece):
    return jnp.sum(piece[HALF:PIECE].astype(F32), axis=0, keepdims=True)


class Scan:
    def __init__(self, place, reverse, refs):
        self.x, self.z, self.c, self.y = place
        self.reverse = reverse
        (self.psend, self.precv, self.gsend, self.zrecv, self.xsend, self.xrecv, self.bsend, self.brecv, self.sem) = refs
        self.group = self.z // ZG
        self.me = lax.rem(self.z, ZG) * NC + self.c

    def device(self, x, z, c):
        return {"seq": x * (NZ * NC) + z * NC + c, "head": self.y}

    def member(self, m):
        return self.device(self.x, self.group * ZG + m // NC, lax.rem(m, NC))

    def copy(self, src, dst, exchange, where):
        return pltpu.make_async_remote_copy(src, dst, self.sem.at[2 * exchange], self.sem.at[2 * exchange + 1],
                                            device_id=where, device_id_type=MESH)

    def all_of(self, exchange):
        ref = (self.precv.at[0:MEMBERS - 1], self.zrecv.at[0:GROUPS - 1], self.xrecv.at[0:NX - 1],
               self.brecv.at[0:(MEMBERS - 1) * HALF])[exchange]
        return self.copy(ref, ref, exchange, self.member(lax.rem(self.me + 1, MEMBERS)))

    def put(self, head, summary, log_total):
        tile = log_tile(log_total)
        data = summary.astype(BF16)
        for half in range(2):
            self.psend[2 * head + half, 0:HALF, :] = data[half * HALF:(half + 1) * HALF]
            self.psend[2 * head + half, HALF:PIECE, :] = tile

    def start_pieces(self):
        for k in (4, 3, 5, 2, 6, 1, 7):
            to = lax.rem(self.me + k, MEMBERS)
            self.copy(self.psend.at[to], self.precv.at[self.me], 0, self.member(to)).start()
        self.precv[self.me] = self.psend[self.me]

    def wait_pieces(self):
        self.all_of(0).wait_recv()

    def order(self, count):
        return reversed(range(count)) if self.reverse else range(count)

    def start_groups(self):
        total = jnp.zeros((HALF, HW), F32)
        log_total = jnp.zeros((1, HW), F32)
        for m in self.order(MEMBERS):
            piece = self.precv[m]
            log_m = log_of(piece)
            total = jnp.exp(log_m) * total + piece[0:HALF].astype(F32)
            log_total = log_total + log_m
        self.gsend[0:HALF, :] = total.astype(BF16)
        self.gsend[HALF:PIECE, :] = log_tile(log_total)
        for k in range(1, GROUPS):
            to = lax.rem(self.group + k, GROUPS)
            self.copy(self.gsend, self.zrecv.at[self.group], 1,
                      self.device(self.x, to * ZG + lax.rem(self.z, ZG), self.c)).start()
        self.zrecv[self.group] = self.gsend[...]

    def prefix(self, recv, count, place):
        before = jnp.zeros((HALF, HW), F32)
        log_before = jnp.zeros((1, HW), F32)
        total = jnp.zeros((HALF, HW), F32)
        log_total = jnp.zeros((1, HW), F32)
        for m in self.order(count):
            before = jnp.where(place == m, total, before)
            log_before = jnp.where(place == m, log_total, log_before)
            piece = recv[m]
            log_m = log_of(piece)
            total = jnp.exp(log_m) * total + piece[0:HALF].astype(F32)
            log_total = log_total + log_m
        return before, log_before, total, log_total

    def wait_groups(self):
        self.all_of(1).wait_recv()

    def start_planes(self):
        self.before, self.log_before, total, log_total = self.prefix(self.zrecv, GROUPS, self.group)
        self.xsend[0:HALF, :] = total.astype(BF16)
        self.xsend[HALF:PIECE, :] = log_tile(log_total)
        for k in (2, 1, 3):
            to = lax.rem(self.x + k, NX)
            self.copy(self.xsend, self.xrecv.at[self.x], 2, self.device(to, self.z, self.c)).start()
        self.xrecv[self.x] = self.xsend[...]

    def wait_planes(self):
        self.all_of(2).wait_recv()

    def start_back(self):
        entering, _, _, _ = self.prefix(self.xrecv, NX, self.x)
        state = jnp.exp(self.log_before) * entering + self.before
        for m in self.order(MEMBERS):
            self.bsend[m] = state.astype(BF16)
            piece = self.precv[m]
            state = jnp.exp(log_of(piece)) * state + piece[0:HALF].astype(F32)
        rows = pl.ds(pl.multiple_of(self.me * HALF, HALF), HALF)
        for k in (4, 3, 5, 2, 6, 1, 7):
            to = lax.rem(self.me + k, MEMBERS)
            self.copy(self.bsend.at[to], self.brecv.at[rows], 3, self.member(to)).start()
        self.brecv[rows, :] = self.bsend[self.me]

    def wait_back(self):
        self.all_of(3).wait_recv()

    def finish(self):
        for exchange in range(4):
            self.all_of(exchange).wait_send()


SCAN_BUFFERS = [
    pltpu.VMEM((MEMBERS, PIECE, HW), BF16),
    pltpu.VMEM((MEMBERS, PIECE, HW), BF16),
    pltpu.VMEM((PIECE, HW), BF16),
    pltpu.VMEM((GROUPS, PIECE, HW), BF16),
    pltpu.VMEM((PIECE, HW), BF16),
    pltpu.VMEM((NX, PIECE, HW), BF16),
    pltpu.VMEM((MEMBERS, HALF, HW), BF16),
    pltpu.VMEM((NH * HW, HW), BF16),
    pltpu.SemaphoreType.DMA((8,)),
]
NB = len(SCAN_BUFFERS)


def kernel(q_hbm, k_hbm, v_hbm, codes_hbm, w_hbm, og_hbm, mixed_out, qg_out, kg_out, vg_out, *scratch):
    fwd_refs, bwd_refs, rest = scratch[:NB], scratch[NB:2 * NB], scratch[2 * NB:]
    (q_ref, k_ref, v_ref, codes_ref, w_ref, og_ref, in_sem, ag, ag_sem, rs_send, rs_recv, rs_sem,
     attn_s, kfall_s, qrise_s, grad_s, out_s, qg_s, kg_s, vg_s, rise_s, fall_s,
     mixed_ref, qg_ref, kg_ref, vg_ref, out_sem) = rest
    seq, y = lax.axis_index("seq"), lax.axis_index("head")
    x, z, c = seq // (NZ * NC), lax.rem(seq, NZ * NC) // NC, lax.rem(seq, NC)
    place = (x, z, c, y)
    fwd, bwd = Scan(place, False, fwd_refs), Scan(place, True, bwd_refs)

    codes_copy, k_copy, v_copy, og_copy, q_copy, w_copy = [
        pltpu.make_async_copy(src, dst, in_sem.at[i])
        for i, (src, dst) in enumerate(((codes_hbm, codes_ref), (k_hbm, k_ref), (v_hbm, v_ref), (og_hbm, og_ref),
                                        (q_hbm, q_ref), (w_hbm, w_ref)))
    ]
    codes_copy.start()

    def row(offset):
        return {"seq": seq, "head": lax.rem(y + NY + offset, NY)}

    barrier = pltpu.get_barrier_semaphore()
    greeted = [fwd.member(lax.rem(fwd.me + k, MEMBERS)) for k in range(1, MEMBERS)]
    greeted += [fwd.device(x, lax.rem(z + k * ZG, NZ), c) for k in range(1, GROUPS)]
    greeted += [fwd.device(lax.rem(x + k, NX), z, c) for k in range(1, NX)]
    greeted += [row(k) for k in (1, -1, 2, -2)]
    for where in greeted:
        pl.semaphore_signal(barrier, inc=1, device_id=where, device_id_type=MESH)
    for copy in (k_copy, v_copy, og_copy, q_copy, w_copy):
        copy.start()

    with scope("wait_codes"):
        codes_copy.wait()
    logs = jnp.log(1.0 - codes_ref[...].astype(F32) * (1.0 / 4096.0))
    ri = lax.broadcasted_iota(jnp.int32, (TOK, TOK), 0)
    ci = lax.broadcasted_iota(jnp.int32, (TOK, TOK), 1)
    lower = ri >= ci
    log_pad = jnp.zeros((TOK, TOK), F32)
    for h in range(NH):
        log_pad = jnp.where(ri == h, logs[h:h + 1, :], log_pad)
    cum_t = lax.dot_general(log_pad, (ri <= ci).astype(F32), (((1,), (0,)), ((), ())),
                            precision=lax.Precision.HIGHEST, preferred_element_type=F32)
    cum = cum_t.T
    with scope("wait_kv"):
        k_copy.wait()
        v_copy.wait()
    heads = [slice(h * HW, (h + 1) * HW) for h in range(NH)]
    for h in range(NH):
        column = jnp.broadcast_to(cum[:, h:h + 1], (TOK, HW))
        last = column[TOK - 1:TOK]
        fall = jnp.exp(last - column)
        fall_s[h] = fall
        rise_s[h] = jnp.exp(column) * SCALE
        k_fall = (fall * k_ref[:, heads[h]].astype(F32)).astype(BF16)
        kfall_s[:, heads[h]] = k_fall
        fwd.put(h, tn(k_fall, v_ref[:, heads[h]]), last)

    with scope("wait_barrier"):
        og_copy.wait()
        pl.semaphore_wait(barrier, len(greeted))
    top, bottom, every = slice(0, HALF), slice(HALF, TOK), slice(0, TOK)

    def ag_copy(owner, rows, i, where, src=None):
        src = ag.at[owner, rows] if src is None else src
        return pltpu.make_async_remote_copy(src, ag.at[owner, rows], ag_sem.at[0], ag_sem.at[i],
                                            device_id=where, device_id_type=MESH)

    def ag_wait(i, owner, rows=every):
        ag_copy(owner, rows, i, row(1)).wait_recv()

    def at(offset):
        return lax.rem(y + NY + offset, NY)

    for i, rows in ((1, top), (3, bottom)):
        for j, sign in enumerate((1, -1)):
            ag_copy(y, rows, i + j, row(2 * sign), og_ref.at[rows]).start()
    fwd.start_pieces()

    q_copy.wait()
    masks = []
    for h in range(NH):
        column = jnp.broadcast_to(cum[:, h:h + 1], (TOK, TOK))
        gap = column - cum_t[h:h + 1, :]
        mask = jnp.where(lower, jnp.exp(jnp.where(lower, gap, 0.0)), 0.0) * SCALE
        masks.append(mask)
        q_h, k_h, v_h = q_ref[:, heads[h]], k_ref[:, heads[h]], v_ref[:, heads[h]]
        attn = (nt(q_h, k_h) * mask).astype(BF16)
        attn_s[h] = attn
        qrise_s[:, heads[h]] = (rise_s[h] * q_h.astype(F32)).astype(BF16)
        out_s[:, heads[h]] = nn(attn, v_h)

    for j, sign in enumerate((1, -1)):
        ag_copy(y, every, 5 + j, row(sign), og_ref).start()
    with scope("wait_w"):
        w_copy.wait()

    def w_cols(owner):
        return w_ref[:, pl.ds(pl.multiple_of(owner * COLS, 128), COLS)]

    grad_s[...] = nt(og_ref[...], w_cols(y))

    def add_grad(offset):
        grad_s[...] += nt(ag[at(offset)], w_cols(at(offset)))

    with scope("wait_pieces_fwd"):
        fwd.wait_pieces()
    fwd.start_groups()
    for i, rows in ((1, top), (3, bottom)):
        for j, sign in enumerate((1, -1)):
            owner = at(-2 * sign)
            with scope("wait_ag2"):
                ag_wait(i + j, owner, rows)
            if (rows == top) == (sign == 1):
                ag_copy(owner, rows, 9, row(2 * sign)).start()
            ag_copy(owner, rows, 7 + j, row(sign)).start()
    add_grad(2)
    add_grad(-2)
    for j, sign in enumerate((1, -1)):
        with scope("wait_ag1"):
            ag_wait(5 + j, at(-sign))
        add_grad(-sign)
    with scope("wait_groups_fwd"):
        fwd.wait_groups()
    fwd.start_planes()
    for j, sign in enumerate((1, -1)):
        with scope("wait_ag3"):
            ag_wait(7 + j, at(-3 * sign))
        add_grad(-3 * sign)
    with scope("wait_ag4"):
        ag_wait(9, at(4))
    add_grad(4)
    for h in range(NH):
        last = jnp.broadcast_to(cum[TOK - 1:TOK, h:h + 1], (1, HW))
        bwd.put(h, tn(qrise_s[:, heads[h]], grad_s[:, heads[h]].astype(BF16)), last)
    bwd.start_pieces()
    with scope("wait_planes_fwd"):
        fwd.wait_planes()
    fwd.start_back()

    for h in range(NH):
        g_h = grad_s[:, heads[h]].astype(BF16)
        q_h, k_h, v_h = q_ref[:, heads[h]], k_ref[:, heads[h]], v_ref[:, heads[h]]
        pmat = (nt(g_h, v_h) * masks[h]).astype(BF16)
        qg_s[:, heads[h]] = nn(pmat, k_h)
        kg_s[:, heads[h]] = tn(pmat, q_h)
        vg_s[:, heads[h]] = tn(attn_s[h], g_h)

    with scope("wait_pieces_bwd"):
        bwd.wait_pieces()
    bwd.start_groups()

    with scope("wait_back_fwd"):
        fwd.wait_back()
    for h in range(NH):
        out_s[:, heads[h]] += nn(qrise_s[:, heads[h]], fwd.brecv[heads[h], :])
    attn_out = out_s[...].astype(BF16)

    def part(offset):
        return nn(attn_out, w_cols(lax.rem(y + NY + offset, NY)))

    out_copies = [pltpu.make_async_copy(src, dst, out_sem.at[i]) for i, (src, dst) in enumerate(
        ((mixed_ref, mixed_out), (qg_ref, qg_out), (kg_ref, kg_out), (vg_ref, vg_out)))]

    def rs_copy(slot, rows, i, where):
        return pltpu.make_async_remote_copy(rs_send.at[slot, rows], rs_recv.at[slot, rows], rs_sem.at[0], rs_sem.at[i],
                                            device_id=where, device_id_type=MESH)

    ways = ((1, bottom, top), (-1, top, bottom))
    for j, (sign, first, second) in enumerate(ways):
        rs_send[j] = part(3 * sign).astype(BF16)
        rs_copy(j, first, 1 + j, row(sign)).start()
    rs_send[2] = part(4).astype(BF16)
    for j, (sign, first, second) in enumerate(ways):
        rs_copy(2, second, 3 + j, row(2 * sign)).start()
        rs_copy(j, second, 3 + j, row(sign)).start()
    for j, (sign, first, second) in enumerate(ways):
        rs_send[3 + j] = part(sign).astype(BF16)
        rs_copy(3 + j, every, 5, row(sign)).start()
    onward = [part(2 * sign) for sign, _, _ in ways]
    own = part(0)

    with scope("wait_groups_bwd"):
        bwd.wait_groups()
    bwd.start_planes()

    for j, (sign, first, second) in enumerate(ways):
        with scope("wait_rs3"):
            rs_copy(j, first, 1 + j, row(sign)).wait_recv()
        rs_send[5 + j, first] = (onward[j][first] + rs_recv[j, first].astype(F32)).astype(BF16)
        rs_copy(5 + j, first, 5, row(2 * sign)).start()
    for j, (sign, first, second) in enumerate(ways):
        with scope("wait_rs4"):
            rs_copy(j, every, 3 + j, row(sign)).wait_recv()
        rs_send[5 + j, second] = (onward[j][second] + rs_recv[j, second].astype(F32)
                                  + rs_recv[2, second].astype(F32)).astype(BF16)
        rs_copy(5 + j, second, 5, row(2 * sign)).start()

    with scope("wait_planes_bwd"):
        bwd.wait_planes()
    bwd.start_back()

    for h in range(NH):
        g_rise = (rise_s[h] * grad_s[:, heads[h]].astype(BF16).astype(F32)).astype(BF16)
        qg_ref[:, heads[h]] = (qg_s[:, heads[h]] + nt(g_rise, fwd.brecv[heads[h], :])).astype(BF16)
    out_copies[1].start()

    with scope("wait_back_bwd"):
        bwd.wait_back()
    for h in range(NH):
        carry = bwd.brecv[heads[h], :]
        v_fall = (fall_s[h] * v_ref[:, heads[h]].astype(F32)).astype(BF16)
        kg_ref[:, heads[h]] = (kg_s[:, heads[h]] + nt(v_fall, carry)).astype(BF16)
        vg_ref[:, heads[h]] = (vg_s[:, heads[h]] + nn(kfall_s[:, heads[h]], carry)).astype(BF16)
    out_copies[2].start()
    out_copies[3].start()

    with scope("wait_rs2"):
        pltpu.make_async_remote_copy(rs_send.at[3:7], rs_recv.at[3:7], rs_sem.at[0], rs_sem.at[5],
                                     device_id=row(1), device_id_type=MESH).wait_recv()
    total = own
    for slot in (3, 4, 5, 6):
        total = total + rs_recv[slot].astype(F32)
    mixed_ref[...] = total.astype(BF16)
    out_copies[0].start()

    with scope("wait_sends"):
        fwd.finish()
        bwd.finish()
        pltpu.make_async_remote_copy(ag.at[0:7], ag.at[0:7], ag_sem.at[0], ag_sem.at[1],
                                     device_id=row(1), device_id_type=MESH).wait_send()
        pltpu.make_async_remote_copy(rs_send, rs_recv, rs_sem.at[0], rs_sem.at[1],
                                     device_id=row(1), device_id_type=MESH).wait_send()
    with scope("wait_out"):
        for copy in out_copies:
            copy.wait()


def store(*refs):
    sources, targets, sem = refs[:4], refs[4:8], refs[8]
    copies = [pltpu.make_async_copy(src, dst, sem.at[i]) for i, (src, dst) in enumerate(zip(sources, targets))]
    for copy in copies:
        copy.start()
    for copy in copies:
        copy.wait()


def local(queries, keys, values, decay_codes, out_weight, out_grad):
    vmem = pl.BlockSpec(memory_space=pltpu.VMEM)
    wide = NH * HW
    placed = [
        pltpu.with_memory_space_constraint(array, pltpu.HBM)
        for array in (queries, keys, values, decay_codes.T, out_weight, out_grad)
    ]
    results = pl.pallas_call(
        kernel,
        out_shape=(
            pltpu.VMEM((TOK, COLS), BF16),
            pltpu.VMEM((TOK, wide), BF16),
            pltpu.VMEM((TOK, wide), BF16),
            pltpu.VMEM((TOK, wide), BF16),
        ),
        in_specs=[pl.BlockSpec(memory_space=pltpu.HBM)] * 6,
        out_specs=(pl.BlockSpec(memory_space=pl.ANY),) * 4,
        scratch_shapes=SCAN_BUFFERS + SCAN_BUFFERS + [
            pltpu.VMEM((TOK, wide), BF16),
            pltpu.VMEM((TOK, wide), BF16),
            pltpu.VMEM((TOK, wide), BF16),
            pltpu.VMEM((NH, TOK), jnp.int32),
            pltpu.VMEM(out_weight.shape, BF16),
            pltpu.VMEM((TOK, COLS), BF16),
            pltpu.SemaphoreType.DMA((6,)),
            pltpu.VMEM((NY, TOK, COLS), BF16),
            pltpu.SemaphoreType.DMA((10,)),
            pltpu.VMEM((7, TOK, COLS), BF16),
            pltpu.VMEM((7, TOK, COLS), BF16),
            pltpu.SemaphoreType.DMA((6,)),
            pltpu.VMEM((NH, TOK, TOK), BF16),
            pltpu.VMEM((TOK, wide), BF16),
            pltpu.VMEM((TOK, wide), BF16),
            pltpu.VMEM((TOK, wide), F32),
            pltpu.VMEM((TOK, wide), F32),
            pltpu.VMEM((TOK, wide), F32),
            pltpu.VMEM((TOK, wide), F32),
            pltpu.VMEM((TOK, wide), F32),
            pltpu.VMEM((NH, TOK, HW), F32),
            pltpu.VMEM((NH, TOK, HW), F32),
            pltpu.VMEM((TOK, COLS), BF16),
            pltpu.VMEM((TOK, wide), BF16),
            pltpu.VMEM((TOK, wide), BF16),
            pltpu.VMEM((TOK, wide), BF16),
            pltpu.SemaphoreType.DMA((4,)),
        ],
        name="linear_attention",
        compiler_params=pltpu.CompilerParams(
            collective_id=0, has_side_effects=True, vmem_limit_bytes=40 * 1024 * 1024
        ),
    )(*placed)
    return pl.pallas_call(
        store,
        out_shape=tuple(jax.ShapeDtypeStruct(array.shape, array.dtype) for array in results),
        in_specs=[vmem] * 4,
        out_specs=tuple([pl.BlockSpec(memory_space=pltpu.HBM)] * 4),
        scratch_shapes=[pltpu.SemaphoreType.DMA((4,))],
        name="store",
    )(*[pltpu.with_memory_space_constraint(array, pltpu.VMEM) for array in results])


def solution(mesh):
    placed = (
        P("seq", "head"),
        P("seq", "head"),
        P("seq", "head"),
        P("seq", "head"),
        P("head", None),
        P("seq", "head"),
    )
    return jax.shard_map(
        local,
        mesh=mesh,
        in_specs=placed,
        out_specs=(P("seq", "head"), P("seq", "head"), P("seq", "head"), P("seq", "head")),
        check_vma=False,
    )
```

```python
import contextlib

import jax
import jax.numpy as jnp
from jax import lax
from jax.experimental import pallas as pl
from jax.experimental.pallas import tpu as pltpu
from jax.sharding import PartitionSpec as P

MESH = pl.DeviceIdType.MESH
BF16 = jnp.bfloat16
F32 = jnp.float32
NX, NZ, NC, NY = 4, 12, 2, 8
ZG = 4
GROUPS = NZ // ZG
MEMBERS = ZG * NC
TOK = 128
HW = 128
NH = 4
COLS = 384
HALF = HW // 2
PIECE = HALF + 16
SCALE = 1.0 / HW
AG_PARTS = 2
RS_PARTS = 2
TRACE = False


def scope(name):
    return jax.named_scope(name) if TRACE else contextlib.nullcontext()


def nn(a, b):
    return lax.dot_general(a, b, (((1,), (0,)), ((), ())), preferred_element_type=F32)


def nt(a, b):
    return lax.dot_general(a, b, (((1,), (1,)), ((), ())), preferred_element_type=F32)


def tn(a, b):
    return lax.dot_general(a, b, (((0,), (0,)), ((), ())), preferred_element_type=F32)


def log_tile(log_total):
    high = log_total.astype(BF16)
    rest = log_total - high.astype(F32)
    mid = rest.astype(BF16)
    low = (rest - mid.astype(F32)).astype(BF16)
    row = lax.broadcasted_iota(jnp.int32, (16, HW), 0)
    parts = [jnp.broadcast_to(part.astype(F32), (16, HW)) for part in (high, mid, low)]
    tile = jnp.where(row == 0, parts[0], jnp.where(row == 1, parts[1], jnp.where(row == 2, parts[2], 0.0)))
    return tile.astype(BF16)


def log_of(ref, m):
    return jnp.sum(ref[m, HALF:PIECE].astype(F32), axis=0, keepdims=True)


class Scan:
    def __init__(self, place, reverse, refs, other=None):
        self.x, self.z, self.c, self.y = place
        self.reverse = reverse
        self.decays = other or self
        (self.psend, self.precv, self.gsend, self.zrecv, self.xsend, self.xrecv, self.bsend, self.brecv, self.sem) = refs
        self.group = self.z // ZG
        self.me = lax.rem(self.z, ZG) * NC + self.c

    def device(self, x, z, c):
        return {"seq": x * (NZ * NC) + z * NC + c, "head": self.y}

    def member(self, m):
        return self.device(self.x, self.group * ZG + m // NC, lax.rem(m, NC))

    def copy(self, src, dst, exchange, where):
        return pltpu.make_async_remote_copy(src, dst, self.sem.at[2 * exchange], self.sem.at[2 * exchange + 1],
                                            device_id=where, device_id_type=MESH)

    def all_of(self, exchange):
        ref = (self.precv.at[0:MEMBERS - 1], self.zrecv.at[0:GROUPS - 1], self.xrecv.at[0:NX - 1],
               self.brecv.at[0:(MEMBERS - 1) * HALF])[exchange]
        return self.copy(ref, ref, exchange, self.member(lax.rem(self.me + 1, MEMBERS)))

    def put(self, head, summary, log_total):
        data = summary.astype(BF16)
        for half in range(2):
            self.psend[2 * head + half, 0:HALF, :] = data[half * HALF:(half + 1) * HALF]
            if self.decays is self:
                self.psend[2 * head + half, HALF:PIECE, :] = log_tile(log_total)

    def start_pieces(self):
        for k in (4, 3, 5, 2, 6, 1, 7):
            to = lax.rem(self.me + k, MEMBERS)
            self.copy(self.psend.at[to], self.precv.at[self.me], 0, self.member(to)).start()
        self.precv[self.me] = self.psend[self.me]

    def wait_pieces(self):
        self.all_of(0).wait_recv()

    def order(self, count):
        return reversed(range(count)) if self.reverse else range(count)

    def start_groups(self):
        total = jnp.zeros((HALF, HW), F32)
        log_total = jnp.zeros((1, HW), F32)
        for m in self.order(MEMBERS):
            log_m = log_of(self.decays.precv, m)
            total = jnp.exp(log_m) * total + self.precv[m, 0:HALF].astype(F32)
            log_total = log_total + log_m
        self.gsend[0:HALF, :] = total.astype(BF16)
        if self.decays is self:
            self.gsend[HALF:PIECE, :] = log_tile(log_total)
        for k in range(1, GROUPS):
            to = lax.rem(self.group + k, GROUPS)
            self.copy(self.gsend, self.zrecv.at[self.group], 1,
                      self.device(self.x, to * ZG + lax.rem(self.z, ZG), self.c)).start()
        self.zrecv[self.group] = self.gsend[...]

    def prefix(self, recv, decays, count, place):
        before = jnp.zeros((HALF, HW), F32)
        log_before = jnp.zeros((1, HW), F32)
        total = jnp.zeros((HALF, HW), F32)
        log_total = jnp.zeros((1, HW), F32)
        for m in self.order(count):
            before = jnp.where(place == m, total, before)
            log_before = jnp.where(place == m, log_total, log_before)
            log_m = log_of(decays, m)
            total = jnp.exp(log_m) * total + recv[m, 0:HALF].astype(F32)
            log_total = log_total + log_m
        return before, log_before, total, log_total

    def wait_groups(self):
        self.all_of(1).wait_recv()

    def start_planes(self):
        self.before, self.log_before, total, log_total = self.prefix(
            self.zrecv, self.decays.zrecv, GROUPS, self.group)
        self.xsend[0:HALF, :] = total.astype(BF16)
        if self.decays is self:
            self.xsend[HALF:PIECE, :] = log_tile(log_total)
        for k in (2, 1, 3):
            to = lax.rem(self.x + k, NX)
            self.copy(self.xsend, self.xrecv.at[self.x], 2, self.device(to, self.z, self.c)).start()
        self.xrecv[self.x] = self.xsend[...]

    def wait_planes(self):
        self.all_of(2).wait_recv()

    def start_back(self):
        entering, _, _, _ = self.prefix(self.xrecv, self.decays.xrecv, NX, self.x)
        state = jnp.exp(self.log_before) * entering + self.before
        for m in self.order(MEMBERS):
            self.bsend[m] = state.astype(BF16)
            state = jnp.exp(log_of(self.decays.precv, m)) * state + self.precv[m, 0:HALF].astype(F32)
        rows = pl.ds(pl.multiple_of(self.me * HALF, HALF), HALF)
        for k in (4, 3, 5, 2, 6, 1, 7):
            to = lax.rem(self.me + k, MEMBERS)
            self.copy(self.bsend.at[to], self.brecv.at[rows], 3, self.member(to)).start()
        self.brecv[rows, :] = self.bsend[self.me]

    def wait_back(self):
        self.all_of(3).wait_recv()

    def finish(self):
        for exchange in range(4):
            self.all_of(exchange).wait_send()


def scan_buffers(length):
    return [
        pltpu.VMEM((MEMBERS, length, HW), BF16),
        pltpu.VMEM((MEMBERS, length, HW), BF16),
        pltpu.VMEM((length, HW), BF16),
        pltpu.VMEM((GROUPS, length, HW), BF16),
        pltpu.VMEM((length, HW), BF16),
        pltpu.VMEM((NX, length, HW), BF16),
        pltpu.VMEM((MEMBERS, HALF, HW), BF16),
        pltpu.VMEM((NH * HW, HW), BF16),
        pltpu.SemaphoreType.DMA((8,)),
    ]


NB = len(scan_buffers(HALF))


def kernel(q_hbm, k_hbm, v_hbm, codes_hbm, w_hbm, og_hbm, mixed_out, qg_out, kg_out, vg_out, *scratch):
    fwd_refs, bwd_refs, rest = scratch[:NB], scratch[NB:2 * NB], scratch[2 * NB:]
    (q_ref, k_ref, v_ref, codes_ref, w_ref, og_ref, in_sem, ag, ag_sem, rs_send, rs_recv, rs_sem,
     attn_s, kfall_s, qrise_s, grad_s, out_s, qg_s, kg_s, vg_s, rise_s, fall_s,
     mixed_ref, qg_ref, kg_ref, vg_ref, out_sem) = rest
    seq, y = lax.axis_index("seq"), lax.axis_index("head")
    x, z, c = seq // (NZ * NC), lax.rem(seq, NZ * NC) // NC, lax.rem(seq, NC)
    place = (x, z, c, y)
    fwd = Scan(place, False, fwd_refs)
    bwd = Scan(place, True, bwd_refs, fwd)

    codes_copy, k_copy, v_copy, og_copy, q_copy, w_copy = [
        pltpu.make_async_copy(src, dst, in_sem.at[i])
        for i, (src, dst) in enumerate(((codes_hbm, codes_ref), (k_hbm, k_ref), (v_hbm, v_ref), (og_hbm, og_ref),
                                        (q_hbm, q_ref), (w_hbm, w_ref)))
    ]
    codes_copy.start()

    def row(offset):
        return {"seq": seq, "head": lax.rem(y + NY + offset, NY)}

    barrier = pltpu.get_barrier_semaphore()
    greeted = [fwd.member(lax.rem(fwd.me + k, MEMBERS)) for k in (4, 3, 5, 2, 6)]
    greeted += [row(k) for k in (2, -2, 1, -1)]
    greeted += [fwd.member(lax.rem(fwd.me + k, MEMBERS)) for k in (1, 7)]
    greeted += [fwd.device(lax.rem(x + k, NX), z, c) for k in (2, 1, 3)]
    greeted += [fwd.device(x, lax.rem(z + k * ZG, NZ), c) for k in range(1, GROUPS)]
    for where in greeted:
        pl.semaphore_signal(barrier, inc=1, device_id=where, device_id_type=MESH)
    for copy in (k_copy, v_copy, og_copy, q_copy, w_copy):
        copy.start()

    with scope("wait_codes"):
        codes_copy.wait()
    logs = jnp.log(1.0 - codes_ref[...].astype(F32) * (1.0 / 4096.0))
    ri = lax.broadcasted_iota(jnp.int32, (TOK, TOK), 0)
    ci = lax.broadcasted_iota(jnp.int32, (TOK, TOK), 1)
    lower = ri >= ci
    log_pad = jnp.zeros((TOK, TOK), F32)
    for h in range(NH):
        log_pad = jnp.where(ri == h, logs[h:h + 1, :], log_pad)
    cum_t = lax.dot_general(log_pad, (ri <= ci).astype(F32), (((1,), (0,)), ((), ())),
                            precision=lax.Precision.HIGHEST, preferred_element_type=F32)
    cum = cum_t.T
    with scope("wait_kv"):
        k_copy.wait()
        v_copy.wait()
    heads = [slice(h * HW, (h + 1) * HW) for h in range(NH)]
    for h in range(NH):
        column = jnp.broadcast_to(cum[:, h:h + 1], (TOK, HW))
        last = column[TOK - 1:TOK]
        fall = jnp.exp(last - column)
        fall_s[h] = fall
        rise_s[h] = jnp.exp(column) * SCALE
        k_fall = (fall * k_ref[:, heads[h]].astype(F32)).astype(BF16)
        kfall_s[:, heads[h]] = k_fall
        fwd.put(h, tn(k_fall, v_ref[:, heads[h]]), last)

    with scope("wait_barrier"):
        og_copy.wait()
        pl.semaphore_wait(barrier, len(greeted))
    every = slice(0, TOK)

    def ways_of(parts):
        cuts = [slice(i * HALF // parts, (i + 1) * HALF // parts) for i in range(2 * parts)]
        return ((0, 1, cuts[:parts], cuts[parts:]), (1, -1, cuts[parts:], cuts[:parts]))

    ways = ways_of(AG_PARTS)

    def at(offset):
        return lax.rem(y + NY + offset, NY)

    def ag_copy(owner, rows, i, where, src=None):
        src = ag.at[owner, rows] if src is None else src
        return pltpu.make_async_remote_copy(src, ag.at[owner, rows], ag_sem.at[0], ag_sem.at[i],
                                            device_id=where, device_id_type=MESH)

    def ag_wait(i, owner, rows=every):
        ag_copy(owner, rows, i, row(1)).wait_recv()

    def ag_index(step, j, i):
        return 4 + (step * 2 + j) * 2 * AG_PARTS + i

    for i in range(2 * AG_PARTS):
        for j, sign, far, near in ways:
            rows = (far + near)[i]
            ag_copy(y, rows, ag_index(0, j, i), row(sign), og_ref.at[rows]).start()
    fwd.start_pieces()

    q_copy.wait()
    masks = []
    for h in range(NH):
        column = jnp.broadcast_to(cum[:, h:h + 1], (TOK, TOK))
        gap = column - cum_t[h:h + 1, :]
        mask = jnp.where(lower, jnp.exp(jnp.where(lower, gap, 0.0)), 0.0) * SCALE
        masks.append(mask)
        q_h, k_h, v_h = q_ref[:, heads[h]], k_ref[:, heads[h]], v_ref[:, heads[h]]
        attn = (nt(q_h, k_h) * mask).astype(BF16)
        attn_s[h] = attn
        qrise_s[:, heads[h]] = (rise_s[h] * q_h.astype(F32)).astype(BF16)
        out_s[:, heads[h]] = nn(attn, v_h)

    with scope("wait_w"):
        w_copy.wait()

    def w_cols(owner):
        return w_ref[:, pl.ds(pl.multiple_of(owner * COLS, 128), COLS)]

    grad_s[...] = nt(og_ref[...], w_cols(y))

    def add_grad(offset):
        grad_s[...] += nt(ag[at(offset)], w_cols(at(offset)))

    for i in range(2 * AG_PARTS):
        for j, sign, far, near in ways:
            rows = (far + near)[i]
            with scope("wait_ag1"):
                ag_wait(ag_index(0, j, i), at(-sign), rows)
            ag_copy(at(-sign), rows, ag_index(1, j, i), row(sign)).start()
    with scope("wait_pieces_fwd"):
        fwd.wait_pieces()
    fwd.start_groups()
    for i in range(2 * AG_PARTS):
        for j, sign, far, near in ways:
            rows = (far + near)[i]
            with scope("wait_ag2"):
                ag_wait(ag_index(1, j, i), at(-2 * sign), rows)
            if i < AG_PARTS:
                ag_copy(at(-2 * sign), rows, 3, row(2 * sign)).start()
            ag_copy(at(-2 * sign), rows, 1 + j, row(sign)).start()
    for offset in (1, -1, 2, -2):
        add_grad(offset)
    with scope("wait_groups_fwd"):
        fwd.wait_groups()
    fwd.start_planes()
    for j, sign, far, near in ways:
        with scope("wait_ag3"):
            ag_wait(1 + j, at(-3 * sign))
        add_grad(-3 * sign)
    with scope("wait_ag4"):
        ag_wait(3, at(4))
    add_grad(4)
    for h in range(NH):
        last = jnp.broadcast_to(cum[TOK - 1:TOK, h:h + 1], (1, HW))
        bwd.put(h, tn(qrise_s[:, heads[h]], grad_s[:, heads[h]].astype(BF16)), last)
    bwd.start_pieces()
    with scope("wait_planes_fwd"):
        fwd.wait_planes()
    fwd.start_back()

    for h in range(NH):
        g_h = grad_s[:, heads[h]].astype(BF16)
        q_h, k_h, v_h = q_ref[:, heads[h]], k_ref[:, heads[h]], v_ref[:, heads[h]]
        pmat = (nt(g_h, v_h) * masks[h]).astype(BF16)
        qg_s[:, heads[h]] = nn(pmat, k_h)
        kg_s[:, heads[h]] = tn(pmat, q_h)
        vg_s[:, heads[h]] = tn(attn_s[h], g_h)

    with scope("wait_pieces_bwd"):
        bwd.wait_pieces()
    bwd.start_groups()

    with scope("wait_back_fwd"):
        fwd.wait_back()
    for h in range(NH):
        out_s[:, heads[h]] += nn(qrise_s[:, heads[h]], fwd.brecv[heads[h], :])
    attn_out = out_s[...].astype(BF16)

    def part(offset):
        return nn(attn_out, w_cols(lax.rem(y + NY + offset, NY)))

    out_copies = [pltpu.make_async_copy(src, dst, out_sem.at[i]) for i, (src, dst) in enumerate(
        ((mixed_ref, mixed_out), (qg_ref, qg_out), (kg_ref, kg_out), (vg_ref, vg_out)))]

    def rs_copy(slot, rows, i, where):
        return pltpu.make_async_remote_copy(rs_send.at[slot, rows], rs_recv.at[slot, rows], rs_sem.at[0], rs_sem.at[i],
                                            device_id=where, device_id_type=MESH)

    ways = ways_of(RS_PARTS)

    def rs_index(left, j, i):
        return 2 + ((left - 2) * 2 + j) * 2 * RS_PARTS + i

    def rs_slot(left, j):
        return 0 if left == 4 else 7 - 2 * left + j

    def rs_on(left, i, parts):
        for j, sign, far, near in ways:
            rows, to = (near + far)[i], rs_slot(left, j)
            total = parts[j][rows]
            if left < 3 or i >= RS_PARTS:
                came = rs_slot(left + 1, j)
                with scope("wait_rs%d" % (left + 1)):
                    rs_copy(came, rows, rs_index(left + 1, j, i), row(sign)).wait_recv()
                total = total + rs_recv[came, rows].astype(F32)
            rs_send[to, rows] = total.astype(BF16)
            rs_copy(to, rows, 1 if left == 1 else rs_index(left, j, i), row(sign)).start()

    rs_send[0] = part(4).astype(BF16)
    for i in range(RS_PARTS):
        for j, sign, far, near in ways:
            rs_copy(0, far[i], rs_index(4, j, RS_PARTS + i), row(sign)).start()
    three = [part(3 * sign) for _, sign, _, _ in ways]
    for i in range(RS_PARTS):
        rs_on(3, i, three)
    two = [part(2 * sign) for _, sign, _, _ in ways]
    one = [part(sign) for _, sign, _, _ in ways]
    own = part(0)

    with scope("wait_groups_bwd"):
        bwd.wait_groups()
    bwd.start_planes()

    for i in range(RS_PARTS):
        rs_on(3, RS_PARTS + i, three)
    for i in range(RS_PARTS):
        rs_on(2, i, two)
    for i in range(RS_PARTS):
        if i == RS_PARTS // 2:
            with scope("wait_planes_bwd"):
                bwd.wait_planes()
            bwd.start_back()
        rs_on(2, RS_PARTS + i, two)

    for i in range(2 * RS_PARTS):
        rs_on(1, i, one)

    for h in range(NH):
        g_rise = (rise_s[h] * grad_s[:, heads[h]].astype(BF16).astype(F32)).astype(BF16)
        qg_ref[:, heads[h]] = (qg_s[:, heads[h]] + nt(g_rise, fwd.brecv[heads[h], :])).astype(BF16)
    out_copies[1].start()

    with scope("wait_back_bwd"):
        bwd.wait_back()
    for h in range(NH):
        carry = bwd.brecv[heads[h], :]
        v_fall = (fall_s[h] * v_ref[:, heads[h]].astype(F32)).astype(BF16)
        kg_ref[:, heads[h]] = (kg_s[:, heads[h]] + nt(v_fall, carry)).astype(BF16)
        vg_ref[:, heads[h]] = (vg_s[:, heads[h]] + nn(kfall_s[:, heads[h]], carry)).astype(BF16)
    out_copies[2].start()
    out_copies[3].start()

    with scope("wait_rs1"):
        pltpu.make_async_remote_copy(rs_send.at[5:7], rs_recv.at[5:7], rs_sem.at[0], rs_sem.at[1],
                                     device_id=row(1), device_id_type=MESH).wait_recv()
    total = own
    for slot in (5, 6):
        total = total + rs_recv[slot].astype(F32)
    mixed_ref[...] = total.astype(BF16)
    out_copies[0].start()

    with scope("wait_sends"):
        fwd.finish()
        bwd.finish()
        pltpu.make_async_remote_copy(ag.at[0:7], ag.at[0:7], ag_sem.at[0], ag_sem.at[1],
                                     device_id=row(1), device_id_type=MESH).wait_send()
        pltpu.make_async_remote_copy(rs_send, rs_recv, rs_sem.at[0], rs_sem.at[1],
                                     device_id=row(1), device_id_type=MESH).wait_send()
    with scope("wait_out"):
        for copy in out_copies:
            copy.wait()


def store(*refs):
    sources, targets, sem = refs[:4], refs[4:8], refs[8]
    copies = [pltpu.make_async_copy(src, dst, sem.at[i]) for i, (src, dst) in enumerate(zip(sources, targets))]
    for copy in copies:
        copy.start()
    for copy in copies:
        copy.wait()


def local(queries, keys, values, decay_codes, out_weight, out_grad):
    vmem = pl.BlockSpec(memory_space=pltpu.VMEM)
    wide = NH * HW
    placed = [
        pltpu.with_memory_space_constraint(array, pltpu.HBM)
        for array in (queries, keys, values, decay_codes.T, out_weight, out_grad)
    ]
    results = pl.pallas_call(
        kernel,
        out_shape=(
            pltpu.VMEM((TOK, COLS), BF16),
            pltpu.VMEM((TOK, wide), BF16),
            pltpu.VMEM((TOK, wide), BF16),
            pltpu.VMEM((TOK, wide), BF16),
        ),
        in_specs=[pl.BlockSpec(memory_space=pltpu.HBM)] * 6,
        out_specs=(pl.BlockSpec(memory_space=pl.ANY),) * 4,
        scratch_shapes=scan_buffers(PIECE) + scan_buffers(HALF) + [
            pltpu.VMEM((TOK, wide), BF16),
            pltpu.VMEM((TOK, wide), BF16),
            pltpu.VMEM((TOK, wide), BF16),
            pltpu.VMEM((NH, TOK), jnp.int32),
            pltpu.VMEM(out_weight.shape, BF16),
            pltpu.VMEM((TOK, COLS), BF16),
            pltpu.SemaphoreType.DMA((6,)),
            pltpu.VMEM((NY, TOK, COLS), BF16),
            pltpu.SemaphoreType.DMA((4 + 8 * AG_PARTS,)),
            pltpu.VMEM((7, TOK, COLS), BF16),
            pltpu.VMEM((7, TOK, COLS), BF16),
            pltpu.SemaphoreType.DMA((2 + 12 * RS_PARTS,)),
            pltpu.VMEM((NH, TOK, TOK), BF16),
            pltpu.VMEM((TOK, wide), BF16),
            pltpu.VMEM((TOK, wide), BF16),
            pltpu.VMEM((TOK, wide), F32),
            pltpu.VMEM((TOK, wide), F32),
            pltpu.VMEM((TOK, wide), F32),
            pltpu.VMEM((TOK, wide), F32),
            pltpu.VMEM((TOK, wide), F32),
            pltpu.VMEM((NH, TOK, HW), F32),
            pltpu.VMEM((NH, TOK, HW), F32),
            pltpu.VMEM((TOK, COLS), BF16),
            pltpu.VMEM((TOK, wide), BF16),
            pltpu.VMEM((TOK, wide), BF16),
            pltpu.VMEM((TOK, wide), BF16),
            pltpu.SemaphoreType.DMA((4,)),
        ],
        name="linear_attention",
        compiler_params=pltpu.CompilerParams(
            collective_id=0, has_side_effects=True, vmem_limit_bytes=40 * 1024 * 1024
        ),
    )(*placed)
    return pl.pallas_call(
        store,
        out_shape=tuple(jax.ShapeDtypeStruct(array.shape, array.dtype) for array in results),
        in_specs=[vmem] * 4,
        out_specs=tuple([pl.BlockSpec(memory_space=pltpu.HBM)] * 4),
        scratch_shapes=[pltpu.SemaphoreType.DMA((4,))],
        name="store",
    )(*[pltpu.with_memory_space_constraint(array, pltpu.VMEM) for array in results])


def solution(mesh):
    placed = (
        P("seq", "head"),
        P("seq", "head"),
        P("seq", "head"),
        P("seq", "head"),
        P("head", None),
        P("seq", "head"),
    )
    return jax.shard_map(
        local,
        mesh=mesh,
        in_specs=placed,
        out_specs=(P("seq", "head"), P("seq", "head"), P("seq", "head"), P("seq", "head")),
        check_vma=False,
    )
```

```python
import contextlib

import jax
import jax.numpy as jnp
from jax import lax
from jax.experimental import pallas as pl
from jax.experimental.pallas import tpu as pltpu
from jax.sharding import PartitionSpec as P

MESH = pl.DeviceIdType.MESH
BF16 = jnp.bfloat16
F32 = jnp.float32
NX, NZ, NC, NY = 4, 12, 2, 8
ZG = 4
GROUPS = NZ // ZG
MEMBERS = ZG * NC
TOK = 128
HW = 128
NH = 4
COLS = 384
HALF = HW // 2
SCALE = 1.0 / HW
AG_PARTS = 2
RS_PARTS = 4
TRACE = False


def scope(name):
    return jax.named_scope(name) if TRACE else contextlib.nullcontext()


def nn(a, b):
    return lax.dot_general(a, b, (((1,), (0,)), ((), ())), preferred_element_type=F32)


def nt(a, b):
    return lax.dot_general(a, b, (((1,), (1,)), ((), ())), preferred_element_type=F32)


def tn(a, b):
    return lax.dot_general(a, b, (((0,), (0,)), ((), ())), preferred_element_type=F32)


class Scan:
    def __init__(self, place, reverse, refs, other=None):
        self.x, self.z, self.c, self.y = place
        self.reverse = reverse
        self.decays = other or self
        (self.psend, self.precv, self.gsend, self.zrecv, self.xsend, self.xrecv, self.bsend, self.brecv, self.sem) = refs[:9]
        if other is None:
            self.lsend, self.lrecv, self.lgsend, self.lzrecv, self.lxsend, self.lxrecv, self.lsem = refs[9:]
        self.group = self.z // ZG
        self.me = lax.rem(self.z, ZG) * NC + self.c

    def device(self, x, z, c):
        return {"seq": x * (NZ * NC) + z * NC + c, "head": self.y}

    def member(self, m):
        return self.device(self.x, self.group * ZG + m // NC, lax.rem(m, NC))

    def copy(self, src, dst, exchange, where):
        return pltpu.make_async_remote_copy(src, dst, self.sem.at[2 * exchange], self.sem.at[2 * exchange + 1],
                                            device_id=where, device_id_type=MESH)

    def all_of(self, exchange):
        ref = (self.precv.at[0:MEMBERS - 1], self.zrecv.at[0:GROUPS - 1], self.xrecv.at[0:NX - 1],
               self.brecv.at[0:(MEMBERS - 1) * HALF])[exchange]
        return self.copy(ref, ref, exchange, self.member(lax.rem(self.me + 1, MEMBERS)))

    def put(self, head, summary, log_total=None):
        data = summary.astype(BF16)
        for half in range(2):
            self.psend[2 * head + half] = data[half * HALF:(half + 1) * HALF]
        if self.decays is self:
            self.lsend[head] = log_total

    def log_copy(self, src, dst, exchange, where):
        return pltpu.make_async_remote_copy(src, dst, self.lsem.at[2 * exchange], self.lsem.at[2 * exchange + 1],
                                            device_id=where, device_id_type=MESH)

    def all_logs(self, exchange):
        ref = (self.lrecv.at[0:MEMBERS - 1], self.lzrecv.at[0:GROUPS - 1], self.lxrecv.at[0:NX - 1])[exchange]
        return self.log_copy(ref, ref, exchange, self.member(lax.rem(self.me + 1, MEMBERS)))

    def start_pieces(self):
        for k in (4, 3, 5, 2, 6, 1, 7):
            to = lax.rem(self.me + k, MEMBERS)
            self.copy(self.psend.at[to], self.precv.at[self.me], 0, self.member(to)).start()
            if self.decays is self:
                self.log_copy(self.lsend.at[to // 2], self.lrecv.at[self.me], 0, self.member(to)).start()
        self.precv[self.me] = self.psend[self.me]
        if self.decays is self:
            self.lrecv[self.me] = self.lsend[self.me // 2]

    def wait_pieces(self):
        self.all_of(0).wait_recv()
        if self.decays is self:
            self.all_logs(0).wait_recv()

    def order(self, count):
        return reversed(range(count)) if self.reverse else range(count)

    def start_groups(self):
        total = jnp.zeros((HALF, HW), F32)
        log_total = jnp.zeros((1, HW), F32)
        for m in self.order(MEMBERS):
            log_m = self.decays.lrecv[m]
            total = jnp.exp(log_m) * total + self.precv[m].astype(F32)
            log_total = log_total + log_m
        self.gsend[...] = total.astype(BF16)
        if self.decays is self:
            self.lgsend[...] = log_total
        for k in range(1, GROUPS):
            to = lax.rem(self.group + k, GROUPS)
            self.copy(self.gsend, self.zrecv.at[self.group], 1,
                      self.device(self.x, to * ZG + lax.rem(self.z, ZG), self.c)).start()
            if self.decays is self:
                self.log_copy(self.lgsend, self.lzrecv.at[self.group], 1,
                              self.device(self.x, to * ZG + lax.rem(self.z, ZG), self.c)).start()
        self.zrecv[self.group] = self.gsend[...]
        if self.decays is self:
            self.lzrecv[self.group] = self.lgsend[...]

    def prefix(self, recv, decays, count, place):
        before = jnp.zeros((HALF, HW), F32)
        log_before = jnp.zeros((1, HW), F32)
        total = jnp.zeros((HALF, HW), F32)
        log_total = jnp.zeros((1, HW), F32)
        for m in self.order(count):
            before = jnp.where(place == m, total, before)
            log_before = jnp.where(place == m, log_total, log_before)
            log_m = decays[m]
            total = jnp.exp(log_m) * total + recv[m].astype(F32)
            log_total = log_total + log_m
        return before, log_before, total, log_total

    def wait_groups(self):
        self.all_of(1).wait_recv()
        if self.decays is self:
            self.all_logs(1).wait_recv()

    def start_planes(self):
        self.before, self.log_before, total, log_total = self.prefix(
            self.zrecv, self.decays.lzrecv, GROUPS, self.group)
        self.xsend[...] = total.astype(BF16)
        if self.decays is self:
            self.lxsend[...] = log_total
        for k in (2, 1, 3):
            to = lax.rem(self.x + k, NX)
            self.copy(self.xsend, self.xrecv.at[self.x], 2, self.device(to, self.z, self.c)).start()
            if self.decays is self:
                self.log_copy(self.lxsend, self.lxrecv.at[self.x], 2, self.device(to, self.z, self.c)).start()
        self.xrecv[self.x] = self.xsend[...]
        if self.decays is self:
            self.lxrecv[self.x] = self.lxsend[...]

    def wait_planes(self):
        self.all_of(2).wait_recv()
        if self.decays is self:
            self.all_logs(2).wait_recv()

    def start_back(self):
        entering, _, _, _ = self.prefix(self.xrecv, self.decays.lxrecv, NX, self.x)
        state = jnp.exp(self.log_before) * entering + self.before
        for m in self.order(MEMBERS):
            self.bsend[m] = state.astype(BF16)
            state = jnp.exp(self.decays.lrecv[m]) * state + self.precv[m].astype(F32)
        rows = pl.ds(pl.multiple_of(self.me * HALF, HALF), HALF)
        for k in (4, 3, 5, 2, 6, 1, 7):
            to = lax.rem(self.me + k, MEMBERS)
            self.copy(self.bsend.at[to], self.brecv.at[rows], 3, self.member(to)).start()
        self.brecv[rows, :] = self.bsend[self.me]

    def wait_back(self):
        self.all_of(3).wait_recv()

    def finish(self):
        for exchange in range(4):
            self.all_of(exchange).wait_send()
            if self.decays is self and exchange < 3:
                self.all_logs(exchange).wait_send()


STATE_BUFFERS = [
    pltpu.VMEM((MEMBERS, HALF, HW), BF16),
    pltpu.VMEM((MEMBERS, HALF, HW), BF16),
    pltpu.VMEM((HALF, HW), BF16),
    pltpu.VMEM((GROUPS, HALF, HW), BF16),
    pltpu.VMEM((HALF, HW), BF16),
    pltpu.VMEM((NX, HALF, HW), BF16),
    pltpu.VMEM((MEMBERS, HALF, HW), BF16),
    pltpu.VMEM((NH * HW, HW), BF16),
    pltpu.SemaphoreType.DMA((8,)),
]
LOG_BUFFERS = [
    pltpu.VMEM((NH, 1, HW), F32),
    pltpu.VMEM((MEMBERS, 1, HW), F32),
    pltpu.VMEM((1, HW), F32),
    pltpu.VMEM((GROUPS, 1, HW), F32),
    pltpu.VMEM((1, HW), F32),
    pltpu.VMEM((NX, 1, HW), F32),
    pltpu.SemaphoreType.DMA((6,)),
]
NF = len(STATE_BUFFERS) + len(LOG_BUFFERS)
NB = NF + len(STATE_BUFFERS)


def kernel(q_hbm, k_hbm, v_hbm, codes_hbm, w_hbm, og_hbm, mixed_ref, qg_ref, kg_ref, vg_ref, *scratch):
    fwd_refs, bwd_refs, rest = scratch[:NF], scratch[NF:NB], scratch[NB:]
    (q_ref, k_ref, v_ref, codes_ref, w_ref, og_ref, in_sem, ag, ag_sem, rs_send, rs_recv, rs_sem,
     attn_s, kfall_s, qrise_s, grad_s, out_s, qg_s, kg_s, vg_s, rise_s, fall_s, vfall_s) = rest
    seq, y = lax.axis_index("seq"), lax.axis_index("head")
    x, z, c = seq // (NZ * NC), lax.rem(seq, NZ * NC) // NC, lax.rem(seq, NC)
    place = (x, z, c, y)
    fwd = Scan(place, False, fwd_refs)
    bwd = Scan(place, True, bwd_refs, fwd)

    codes_copy, k_copy, v_copy, og_copy, q_copy, w_copy = [
        pltpu.make_async_copy(src, dst, in_sem.at[i])
        for i, (src, dst) in enumerate(((codes_hbm, codes_ref), (k_hbm, k_ref), (v_hbm, v_ref), (og_hbm, og_ref),
                                        (q_hbm, q_ref), (w_hbm, w_ref)))
    ]
    codes_copy.start()

    def row(offset):
        return {"seq": seq, "head": lax.rem(y + NY + offset, NY)}

    barrier = pltpu.get_barrier_semaphore()
    greeted = [fwd.member(lax.rem(fwd.me + k, MEMBERS)) for k in (4, 3, 5, 2, 6)]
    greeted += [row(k) for k in (2, -2, 1, -1)]
    greeted += [fwd.member(lax.rem(fwd.me + k, MEMBERS)) for k in (1, 7)]
    greeted += [fwd.device(lax.rem(x + k, NX), z, c) for k in (2, 1, 3)]
    greeted += [fwd.device(x, lax.rem(z + k * ZG, NZ), c) for k in range(1, GROUPS)]
    for where in greeted:
        pl.semaphore_signal(barrier, inc=1, device_id=where, device_id_type=MESH)
    for copy in (k_copy, v_copy, og_copy, q_copy, w_copy):
        copy.start()

    with scope("wait_codes"):
        codes_copy.wait()
    logs = jnp.log(1.0 - codes_ref[...].astype(F32) * (1.0 / 4096.0))
    ri = lax.broadcasted_iota(jnp.int32, (TOK, TOK), 0)
    ci = lax.broadcasted_iota(jnp.int32, (TOK, TOK), 1)
    lower = ri >= ci
    log_pad = jnp.zeros((TOK, TOK), F32)
    for h in range(NH):
        log_pad = jnp.where(ri == h, logs[h:h + 1, :], log_pad)
    cum_t = lax.dot_general(log_pad, (ri <= ci).astype(F32), (((1,), (0,)), ((), ())),
                            precision=lax.Precision.HIGHEST, preferred_element_type=F32)
    cum = cum_t.T
    with scope("wait_kv"):
        k_copy.wait()
        v_copy.wait()
    heads = [slice(h * HW, (h + 1) * HW) for h in range(NH)]
    for h in range(NH):
        column = jnp.broadcast_to(cum[:, h:h + 1], (TOK, HW))
        last = column[TOK - 1:TOK]
        fall = jnp.exp(last - column)
        fall_s[h] = fall
        rise_s[h] = jnp.exp(column) * SCALE
        k_fall = (fall * k_ref[:, heads[h]].astype(F32)).astype(BF16)
        kfall_s[:, heads[h]] = k_fall
        fwd.put(h, tn(k_fall, v_ref[:, heads[h]]), last)

    with scope("wait_barrier"):
        og_copy.wait()
        pl.semaphore_wait(barrier, len(greeted))
    fwd.start_pieces()
    every = slice(0, TOK)

    def ways_of(parts):
        cuts = [slice(i * HALF // parts, (i + 1) * HALF // parts) for i in range(2 * parts)]
        return ((0, 1, cuts[:parts], cuts[parts:]), (1, -1, cuts[parts:], cuts[:parts]))

    ways = ways_of(AG_PARTS)

    def at(offset):
        return lax.rem(y + NY + offset, NY)

    def ag_copy(owner, rows, i, where, src=None):
        src = ag.at[owner, rows] if src is None else src
        return pltpu.make_async_remote_copy(src, ag.at[owner, rows], ag_sem.at[0], ag_sem.at[i],
                                            device_id=where, device_id_type=MESH)

    def ag_wait(i, owner, rows=every):
        ag_copy(owner, rows, i, row(1)).wait_recv()

    def ag_index(step, j, i):
        return 4 + (step * 2 + j) * 2 * AG_PARTS + i

    for i in range(2 * AG_PARTS):
        for j, sign, far, near in ways:
            rows = (far + near)[i]
            ag_copy(y, rows, ag_index(0, j, i), row(sign), og_ref.at[rows]).start()

    q_copy.wait()
    masks = []
    for h in range(NH):
        column = jnp.broadcast_to(cum[:, h:h + 1], (TOK, TOK))
        gap = column - cum_t[h:h + 1, :]
        mask = jnp.where(lower, jnp.exp(jnp.where(lower, gap, 0.0)), 0.0) * SCALE
        masks.append(mask)
        q_h, k_h, v_h = q_ref[:, heads[h]], k_ref[:, heads[h]], v_ref[:, heads[h]]
        attn = (nt(q_h, k_h) * mask).astype(BF16)
        attn_s[h] = attn
        qrise_s[:, heads[h]] = (rise_s[h] * q_h.astype(F32)).astype(BF16)
        out_s[:, heads[h]] = nn(attn, v_h)

    with scope("wait_w"):
        w_copy.wait()

    def w_cols(owner):
        return w_ref[:, pl.ds(pl.multiple_of(owner * COLS, 128), COLS)]

    grad_s[...] = nt(og_ref[...], w_cols(y))

    def add_grad(offset):
        grad_s[...] += nt(ag[at(offset)], w_cols(at(offset)))

    for i in range(2 * AG_PARTS):
        for j, sign, far, near in ways:
            rows = (far + near)[i]
            with scope("wait_ag1"):
                ag_wait(ag_index(0, j, i), at(-sign), rows)
            ag_copy(at(-sign), rows, ag_index(1, j, i), row(sign)).start()
    with scope("wait_pieces_fwd"):
        fwd.wait_pieces()
    fwd.start_groups()
    for i in range(2 * AG_PARTS):
        for j, sign, far, near in ways:
            rows = (far + near)[i]
            with scope("wait_ag2"):
                ag_wait(ag_index(1, j, i), at(-2 * sign), rows)
            if i < AG_PARTS:
                ag_copy(at(-2 * sign), rows, 3, row(2 * sign)).start()
            ag_copy(at(-2 * sign), rows, 1 + j, row(sign)).start()
    for offset in (1, -1, 2, -2):
        add_grad(offset)
    with scope("wait_groups_fwd"):
        fwd.wait_groups()
    fwd.start_planes()
    for j, sign, far, near in ways:
        with scope("wait_ag3"):
            ag_wait(1 + j, at(-3 * sign))
        add_grad(-3 * sign)
    with scope("wait_ag4"):
        ag_wait(3, at(4))
    add_grad(4)
    for h in range(NH):
        bwd.put(h, tn(qrise_s[:, heads[h]], grad_s[:, heads[h]].astype(BF16)))
    bwd.start_pieces()
    with scope("wait_planes_fwd"):
        fwd.wait_planes()
    fwd.start_back()

    for h in range(NH):
        g_h = grad_s[:, heads[h]].astype(BF16)
        q_h, k_h, v_h = q_ref[:, heads[h]], k_ref[:, heads[h]], v_ref[:, heads[h]]
        pmat = (nt(g_h, v_h) * masks[h]).astype(BF16)
        qg_s[:, heads[h]] = nn(pmat, k_h)
        kg_s[:, heads[h]] = tn(pmat, q_h)
        vg_s[:, heads[h]] = tn(attn_s[h], g_h)
        vfall_s[:, heads[h]] = (fall_s[h] * v_ref[:, heads[h]].astype(F32)).astype(BF16)

    with scope("wait_pieces_bwd"):
        bwd.wait_pieces()
    bwd.start_groups()

    with scope("wait_back_fwd"):
        fwd.wait_back()
    for h in range(NH):
        out_s[:, heads[h]] += nn(qrise_s[:, heads[h]], fwd.brecv[heads[h], :])
    attn_out = out_s[...].astype(BF16)

    def part(offset):
        return nn(attn_out, w_cols(lax.rem(y + NY + offset, NY)))

    def rs_copy(slot, rows, i, where):
        return pltpu.make_async_remote_copy(rs_send.at[slot, rows], rs_recv.at[slot, rows], rs_sem.at[0], rs_sem.at[i],
                                            device_id=where, device_id_type=MESH)

    ways = ways_of(RS_PARTS)

    def rs_index(left, j, i):
        return 2 + ((left - 2) * 2 + j) * 2 * RS_PARTS + i

    def rs_slot(left, j):
        return 0 if left == 4 else 7 - 2 * left + j

    def rs_wait(slot, rows, i):
        with scope("wait_rs%d" % slot):
            rs_copy(slot, rows, i, row(1)).wait_recv()
        return rs_recv[slot, rows].astype(F32)

    def rs_on(left, i, parts):
        for j, sign, far, near in ways:
            rows, to, came = (near + far)[i], rs_slot(left, j), rs_slot(left + 1, j)
            total = parts[j][rows] + rs_wait(came, rows, rs_index(left + 1, j, i))
            if left == 2 and i >= RS_PARTS:
                total = total + rs_wait(0, rows, rs_index(4, j, i))
            rs_send[to, rows] = total.astype(BF16)
            rs_copy(to, rows, 1 if left == 1 else rs_index(left, j, i), row(sign)).start()

    rs_send[0] = part(4).astype(BF16)
    for i in range(RS_PARTS):
        for j, sign, far, near in ways:
            rs_copy(0, far[i], rs_index(4, j, RS_PARTS + i), row(2 * sign)).start()
    for j, sign, far, near in ways:
        rs_send[1 + j] = part(3 * sign).astype(BF16)
        for i in range(RS_PARTS):
            rs_copy(1 + j, far[i], rs_index(3, j, RS_PARTS + i), row(sign)).start()
    for i in range(RS_PARTS):
        for j, sign, far, near in ways:
            rs_copy(1 + j, near[i], rs_index(3, j, i), row(sign)).start()
    two = [part(2 * sign) for _, sign, _, _ in ways]
    one = [part(sign) for _, sign, _, _ in ways]
    own = part(0)

    with scope("wait_groups_bwd"):
        bwd.wait_groups()
    bwd.start_planes()

    for i in range(RS_PARTS):
        rs_on(2, RS_PARTS + i, two)
    for i in range(RS_PARTS):
        rs_on(2, i, two)
    with scope("wait_planes_bwd"):
        bwd.wait_planes()
    bwd.start_back()
    for i in range(RS_PARTS):
        rs_on(1, RS_PARTS + i, one)
    for i in range(RS_PARTS):
        rs_on(1, i, one)

    for h in range(NH):
        g_rise = (rise_s[h] * grad_s[:, heads[h]].astype(BF16).astype(F32)).astype(BF16)
        qg_ref[:, heads[h]] = (qg_s[:, heads[h]] + nt(g_rise, fwd.brecv[heads[h], :])).astype(BF16)

    with scope("wait_back_bwd"):
        bwd.wait_back()
    for h in range(NH):
        carry = bwd.brecv[heads[h], :]
        kg_ref[:, heads[h]] = (kg_s[:, heads[h]] + nt(vfall_s[:, heads[h]], carry)).astype(BF16)
        vg_ref[:, heads[h]] = (vg_s[:, heads[h]] + nn(kfall_s[:, heads[h]], carry)).astype(BF16)

    with scope("wait_rs1"):
        pltpu.make_async_remote_copy(rs_send.at[5:7], rs_recv.at[5:7], rs_sem.at[0], rs_sem.at[1],
                                     device_id=row(1), device_id_type=MESH).wait_recv()
    total = own
    for slot in (5, 6):
        total = total + rs_recv[slot].astype(F32)
    mixed_ref[...] = total.astype(BF16)

    with scope("wait_sends"):
        fwd.finish()
        bwd.finish()
        pltpu.make_async_remote_copy(ag.at[0:7], ag.at[0:7], ag_sem.at[0], ag_sem.at[1],
                                     device_id=row(1), device_id_type=MESH).wait_send()
        pltpu.make_async_remote_copy(rs_send, rs_recv, rs_sem.at[0], rs_sem.at[1],
                                     device_id=row(1), device_id_type=MESH).wait_send()


def store(*refs):
    sources, targets, sem = refs[:4], refs[4:8], refs[8]
    copies = [pltpu.make_async_copy(src, dst, sem.at[i]) for i, (src, dst) in enumerate(zip(sources, targets))]
    for copy in copies:
        copy.start()
    for copy in copies:
        copy.wait()


def local(queries, keys, values, decay_codes, out_weight, out_grad):
    vmem = pl.BlockSpec(memory_space=pltpu.VMEM)
    wide = NH * HW
    placed = [
        pltpu.with_memory_space_constraint(array, pltpu.HBM)
        for array in (queries, keys, values, decay_codes.T, out_weight, out_grad)
    ]
    results = pl.pallas_call(
        kernel,
        out_shape=(
            pltpu.VMEM((TOK, COLS), BF16),
            pltpu.VMEM((TOK, wide), BF16),
            pltpu.VMEM((TOK, wide), BF16),
            pltpu.VMEM((TOK, wide), BF16),
        ),
        in_specs=[pl.BlockSpec(memory_space=pltpu.HBM)] * 6,
        out_specs=(vmem,) * 4,
        scratch_shapes=STATE_BUFFERS + LOG_BUFFERS + STATE_BUFFERS + [
            pltpu.VMEM((TOK, wide), BF16),
            pltpu.VMEM((TOK, wide), BF16),
            pltpu.VMEM((TOK, wide), BF16),
            pltpu.VMEM((NH, TOK), jnp.int32),
            pltpu.VMEM(out_weight.shape, BF16),
            pltpu.VMEM((TOK, COLS), BF16),
            pltpu.SemaphoreType.DMA((6,)),
            pltpu.VMEM((NY, TOK, COLS), BF16),
            pltpu.SemaphoreType.DMA((4 + 8 * AG_PARTS,)),
            pltpu.VMEM((7, TOK, COLS), BF16),
            pltpu.VMEM((7, TOK, COLS), BF16),
            pltpu.SemaphoreType.DMA((2 + 12 * RS_PARTS,)),
            pltpu.VMEM((NH, TOK, TOK), BF16),
            pltpu.VMEM((TOK, wide), BF16),
            pltpu.VMEM((TOK, wide), BF16),
            pltpu.VMEM((TOK, wide), F32),
            pltpu.VMEM((TOK, wide), F32),
            pltpu.VMEM((TOK, wide), F32),
            pltpu.VMEM((TOK, wide), F32),
            pltpu.VMEM((TOK, wide), F32),
            pltpu.VMEM((NH, TOK, HW), F32),
            pltpu.VMEM((NH, TOK, HW), F32),
            pltpu.VMEM((TOK, wide), BF16),
        ],
        name="linear_attention",
        compiler_params=pltpu.CompilerParams(
            collective_id=0, has_side_effects=True, vmem_limit_bytes=40 * 1024 * 1024
        ),
    )(*placed)
    return pl.pallas_call(
        store,
        out_shape=tuple(jax.ShapeDtypeStruct(array.shape, array.dtype) for array in results),
        in_specs=[vmem] * 4,
        out_specs=tuple([pl.BlockSpec(memory_space=pltpu.HBM)] * 4),
        scratch_shapes=[pltpu.SemaphoreType.DMA((4,))],
        name="store",
    )(*[pltpu.with_memory_space_constraint(array, pltpu.VMEM) for array in results])


def solution(mesh):
    placed = (
        P("seq", "head"),
        P("seq", "head"),
        P("seq", "head"),
        P("seq", "head"),
        P("head", None),
        P("seq", "head"),
    )
    return jax.shard_map(
        local,
        mesh=mesh,
        in_specs=placed,
        out_specs=(P("seq", "head"), P("seq", "head"), P("seq", "head"), P("seq", "head")),
        check_vma=False,
    )
```

```python
import contextlib

import jax
import jax.numpy as jnp
from jax import lax
from jax.experimental import pallas as pl
from jax.experimental.pallas import tpu as pltpu
from jax.sharding import PartitionSpec as P

MESH = pl.DeviceIdType.MESH
BF16 = jnp.bfloat16
F32 = jnp.float32
NX, NZ, NC, NY = 4, 12, 2, 8
ZG = 4
GROUPS = NZ // ZG
MEMBERS = ZG * NC
TOK = 128
HW = 128
NH = 4
COLS = 384
HALF = HW // 2
SCALE = 1.0 / HW
AG_PARTS = 2
RS_PARTS = 4
TRACE = False


def scope(name):
    return jax.named_scope(name) if TRACE else contextlib.nullcontext()


def nn(a, b):
    return lax.dot_general(a, b, (((1,), (0,)), ((), ())), preferred_element_type=F32)


def nt(a, b):
    return lax.dot_general(a, b, (((1,), (1,)), ((), ())), preferred_element_type=F32)


def tn(a, b):
    return lax.dot_general(a, b, (((0,), (0,)), ((), ())), preferred_element_type=F32)


class Scan:
    def __init__(self, place, reverse, refs, other=None):
        self.x, self.z, self.c, self.y = place
        self.reverse = reverse
        self.decays = other or self
        (self.psend, self.precv, self.gsend, self.zrecv, self.xsend, self.xrecv, self.bsend, self.brecv, self.sem) = refs[:9]
        if other is None:
            self.lsend, self.lrecv, self.lgsend, self.lzrecv, self.lxsend, self.lxrecv, self.lsem = refs[9:]
        self.group = self.z // ZG
        self.me = lax.rem(self.z, ZG) * NC + self.c

    def device(self, x, z, c):
        return {"seq": x * (NZ * NC) + z * NC + c, "head": self.y}

    def member(self, m):
        return self.device(self.x, self.group * ZG + m // NC, lax.rem(m, NC))

    def copy(self, src, dst, exchange, where):
        return pltpu.make_async_remote_copy(src, dst, self.sem.at[2 * exchange], self.sem.at[2 * exchange + 1],
                                            device_id=where, device_id_type=MESH)

    def all_of(self, exchange):
        ref = (self.precv.at[0:MEMBERS - 1], self.zrecv.at[0:GROUPS - 1], self.xrecv.at[0:NX - 1],
               self.brecv.at[0:(MEMBERS - 1) * HALF])[exchange]
        return self.copy(ref, ref, exchange, self.member(lax.rem(self.me + 1, MEMBERS)))

    def put(self, head, summary, log_total=None):
        data = summary.astype(BF16)
        for half in range(2):
            self.psend[2 * head + half] = data[half * HALF:(half + 1) * HALF]
        if self.decays is self:
            self.lsend[head] = log_total

    def log_copy(self, src, dst, exchange, where):
        return pltpu.make_async_remote_copy(src, dst, self.lsem.at[2 * exchange], self.lsem.at[2 * exchange + 1],
                                            device_id=where, device_id_type=MESH)

    def all_logs(self, exchange):
        ref = (self.lrecv.at[0:MEMBERS - 1], self.lzrecv.at[0:GROUPS - 1], self.lxrecv.at[0:NX - 1])[exchange]
        return self.log_copy(ref, ref, exchange, self.member(lax.rem(self.me + 1, MEMBERS)))

    def start_pieces(self):
        for k in (4, 3, 5, 2, 6, 1, 7):
            to = lax.rem(self.me + k, MEMBERS)
            self.copy(self.psend.at[to], self.precv.at[self.me], 0, self.member(to)).start()
            if self.decays is self:
                self.log_copy(self.lsend.at[to // 2], self.lrecv.at[self.me], 0, self.member(to)).start()
        self.precv[self.me] = self.psend[self.me]
        if self.decays is self:
            self.lrecv[self.me] = self.lsend[self.me // 2]

    def wait_pieces(self):
        self.all_of(0).wait_recv()
        if self.decays is self:
            self.all_logs(0).wait_recv()

    def order(self, count):
        return reversed(range(count)) if self.reverse else range(count)

    def start_groups(self):
        total = jnp.zeros((HALF, HW), F32)
        log_total = jnp.zeros((1, HW), F32)
        for m in self.order(MEMBERS):
            log_m = self.decays.lrecv[m]
            total = jnp.exp(log_m) * total + self.precv[m].astype(F32)
            log_total = log_total + log_m
        self.gsend[...] = total.astype(BF16)
        if self.decays is self:
            self.lgsend[...] = log_total
        for k in range(1, GROUPS):
            to = lax.rem(self.group + k, GROUPS)
            self.copy(self.gsend, self.zrecv.at[self.group], 1,
                      self.device(self.x, to * ZG + lax.rem(self.z, ZG), self.c)).start()
            if self.decays is self:
                self.log_copy(self.lgsend, self.lzrecv.at[self.group], 1,
                              self.device(self.x, to * ZG + lax.rem(self.z, ZG), self.c)).start()
        self.zrecv[self.group] = self.gsend[...]
        if self.decays is self:
            self.lzrecv[self.group] = self.lgsend[...]

    def prefix(self, recv, decays, count, place):
        before = jnp.zeros((HALF, HW), F32)
        log_before = jnp.zeros((1, HW), F32)
        total = jnp.zeros((HALF, HW), F32)
        log_total = jnp.zeros((1, HW), F32)
        for m in self.order(count):
            before = jnp.where(place == m, total, before)
            log_before = jnp.where(place == m, log_total, log_before)
            log_m = decays[m]
            total = jnp.exp(log_m) * total + recv[m].astype(F32)
            log_total = log_total + log_m
        return before, log_before, total, log_total

    def wait_groups(self):
        self.all_of(1).wait_recv()
        if self.decays is self:
            self.all_logs(1).wait_recv()

    def start_planes(self):
        self.before, self.log_before, total, log_total = self.prefix(
            self.zrecv, self.decays.lzrecv, GROUPS, self.group)
        self.xsend[...] = total.astype(BF16)
        if self.decays is self:
            self.lxsend[...] = log_total
        for k in (2, 1, 3):
            to = lax.rem(self.x + k, NX)
            self.copy(self.xsend, self.xrecv.at[self.x], 2, self.device(to, self.z, self.c)).start()
            if self.decays is self:
                self.log_copy(self.lxsend, self.lxrecv.at[self.x], 2, self.device(to, self.z, self.c)).start()
        self.xrecv[self.x] = self.xsend[...]
        if self.decays is self:
            self.lxrecv[self.x] = self.lxsend[...]

    def wait_planes(self):
        self.all_of(2).wait_recv()
        if self.decays is self:
            self.all_logs(2).wait_recv()

    def start_back(self):
        entering, _, _, _ = self.prefix(self.xrecv, self.decays.lxrecv, NX, self.x)
        state = jnp.exp(self.log_before) * entering + self.before
        for m in self.order(MEMBERS):
            self.bsend[m] = state.astype(BF16)
            state = jnp.exp(self.decays.lrecv[m]) * state + self.precv[m].astype(F32)
        rows = pl.ds(pl.multiple_of(self.me * HALF, HALF), HALF)
        for k in (4, 3, 5, 2, 6, 1, 7):
            to = lax.rem(self.me + k, MEMBERS)
            self.copy(self.bsend.at[to], self.brecv.at[rows], 3, self.member(to)).start()
        self.brecv[rows, :] = self.bsend[self.me]

    def wait_back(self):
        self.all_of(3).wait_recv()

    def finish(self):
        for exchange in range(4):
            self.all_of(exchange).wait_send()
            if self.decays is self and exchange < 3:
                self.all_logs(exchange).wait_send()


STATE_BUFFERS = [
    pltpu.VMEM((MEMBERS, HALF, HW), BF16),
    pltpu.VMEM((MEMBERS, HALF, HW), BF16),
    pltpu.VMEM((HALF, HW), BF16),
    pltpu.VMEM((GROUPS, HALF, HW), BF16),
    pltpu.VMEM((HALF, HW), BF16),
    pltpu.VMEM((NX, HALF, HW), BF16),
    pltpu.VMEM((MEMBERS, HALF, HW), BF16),
    pltpu.VMEM((NH * HW, HW), BF16),
    pltpu.SemaphoreType.DMA((8,)),
]
LOG_BUFFERS = [
    pltpu.VMEM((NH, 1, HW), F32),
    pltpu.VMEM((MEMBERS, 1, HW), F32),
    pltpu.VMEM((1, HW), F32),
    pltpu.VMEM((GROUPS, 1, HW), F32),
    pltpu.VMEM((1, HW), F32),
    pltpu.VMEM((NX, 1, HW), F32),
    pltpu.SemaphoreType.DMA((6,)),
]
NF = len(STATE_BUFFERS) + len(LOG_BUFFERS)
NB = NF + len(STATE_BUFFERS)


def kernel(q_hbm, k_hbm, v_hbm, codes_hbm, w_hbm, og_hbm, mixed_ref, qg_ref, kg_ref, vg_ref, *scratch):
    fwd_refs, bwd_refs, rest = scratch[:NF], scratch[NF:NB], scratch[NB:]
    (q_ref, k_ref, v_ref, codes_ref, w_ref, og_ref, in_sem, ag, ag_sem, rs_send, rs_recv, rs_sem,
     attn_s, kfall_s, qrise_s, grad_s, out_s, qg_s, kg_s, vg_s, rise_s, fall_s, vfall_s) = rest
    seq, y = lax.axis_index("seq"), lax.axis_index("head")
    x, z, c = seq // (NZ * NC), lax.rem(seq, NZ * NC) // NC, lax.rem(seq, NC)
    place = (x, z, c, y)
    fwd = Scan(place, False, fwd_refs)
    bwd = Scan(place, True, bwd_refs, fwd)

    codes_copy, k_copy, v_copy, og_copy, q_copy, w_copy = [
        pltpu.make_async_copy(src, dst, in_sem.at[i])
        for i, (src, dst) in enumerate(((codes_hbm, codes_ref), (k_hbm, k_ref), (v_hbm, v_ref), (og_hbm, og_ref),
                                        (q_hbm, q_ref), (w_hbm, w_ref)))
    ]
    codes_copy.start()

    def row(offset):
        return {"seq": seq, "head": lax.rem(y + NY + offset, NY)}

    barrier = pltpu.get_barrier_semaphore()
    greeted = [fwd.member(lax.rem(fwd.me + k, MEMBERS)) for k in (4, 3, 5, 2, 6)]
    greeted += [row(k) for k in (2, -2, 1, -1)]
    greeted += [fwd.member(lax.rem(fwd.me + k, MEMBERS)) for k in (1, 7)]
    greeted += [fwd.device(lax.rem(x + k, NX), z, c) for k in (2, 1, 3)]
    greeted += [fwd.device(x, lax.rem(z + k * ZG, NZ), c) for k in range(1, GROUPS)]
    for where in greeted:
        pl.semaphore_signal(barrier, inc=1, device_id=where, device_id_type=MESH)
    for copy in (k_copy, v_copy, og_copy, q_copy, w_copy):
        copy.start()

    with scope("wait_codes"):
        codes_copy.wait()
    logs = jnp.log(1.0 - codes_ref[...].astype(F32) * (1.0 / 4096.0))
    ri = lax.broadcasted_iota(jnp.int32, (TOK, TOK), 0)
    ci = lax.broadcasted_iota(jnp.int32, (TOK, TOK), 1)
    lower = ri >= ci
    log_pad = jnp.zeros((TOK, TOK), F32)
    for h in range(NH):
        log_pad = jnp.where(ri == h, logs[h:h + 1, :], log_pad)
    cum_t = lax.dot_general(log_pad, (ri <= ci).astype(F32), (((1,), (0,)), ((), ())),
                            precision=lax.Precision.HIGHEST, preferred_element_type=F32)
    cum = cum_t.T
    with scope("wait_kv"):
        k_copy.wait()
        v_copy.wait()
    heads = [slice(h * HW, (h + 1) * HW) for h in range(NH)]
    for h in range(NH):
        column = jnp.broadcast_to(cum[:, h:h + 1], (TOK, HW))
        last = column[TOK - 1:TOK]
        fall = jnp.exp(last - column)
        fall_s[h] = fall
        rise_s[h] = jnp.exp(column) * SCALE
        k_fall = (fall * k_ref[:, heads[h]].astype(F32)).astype(BF16)
        kfall_s[:, heads[h]] = k_fall
        fwd.put(h, tn(k_fall, v_ref[:, heads[h]]), last)

    with scope("wait_barrier"):
        og_copy.wait()
        pl.semaphore_wait(barrier, len(greeted))
    fwd.start_pieces()
    every = slice(0, TOK)

    def ways_of(parts):
        cuts = [slice(i * HALF // parts, (i + 1) * HALF // parts) for i in range(2 * parts)]
        return ((0, 1, cuts[:parts], cuts[parts:]), (1, -1, cuts[parts:], cuts[:parts]))

    ways = ways_of(AG_PARTS)

    def at(offset):
        return lax.rem(y + NY + offset, NY)

    def ag_copy(owner, rows, i, where, src=None):
        src = ag.at[owner, rows] if src is None else src
        return pltpu.make_async_remote_copy(src, ag.at[owner, rows], ag_sem.at[0], ag_sem.at[i],
                                            device_id=where, device_id_type=MESH)

    def ag_wait(i, owner, rows=every):
        ag_copy(owner, rows, i, row(1)).wait_recv()

    def ag_index(step, j, i):
        return 4 + (step * 2 + j) * 2 * AG_PARTS + i

    for i in range(2 * AG_PARTS):
        for j, sign, far, near in ways:
            rows = (far + near)[i]
            ag_copy(y, rows, ag_index(0, j, i), row(sign), og_ref.at[rows]).start()

    q_copy.wait()
    masks = []
    for h in range(NH):
        column = jnp.broadcast_to(cum[:, h:h + 1], (TOK, TOK))
        gap = column - cum_t[h:h + 1, :]
        mask = jnp.where(lower, jnp.exp(jnp.where(lower, gap, 0.0)), 0.0) * SCALE
        masks.append(mask)
        q_h, k_h, v_h = q_ref[:, heads[h]], k_ref[:, heads[h]], v_ref[:, heads[h]]
        attn = (nt(q_h, k_h) * mask).astype(BF16)
        attn_s[h] = attn
        qrise_s[:, heads[h]] = (rise_s[h] * q_h.astype(F32)).astype(BF16)
        out_s[:, heads[h]] = nn(attn, v_h)

    with scope("wait_w"):
        w_copy.wait()

    def w_cols(owner):
        return w_ref[:, pl.ds(pl.multiple_of(owner * COLS, 128), COLS)]

    grad_s[...] = nt(og_ref[...], w_cols(y))

    def add_grad(offset):
        grad_s[...] += nt(ag[at(offset)], w_cols(at(offset)))

    for i in range(2 * AG_PARTS):
        for j, sign, far, near in ways:
            rows = (far + near)[i]
            with scope("wait_ag1"):
                ag_wait(ag_index(0, j, i), at(-sign), rows)
            ag_copy(at(-sign), rows, ag_index(1, j, i), row(sign)).start()
    with scope("wait_pieces_fwd"):
        fwd.wait_pieces()
    fwd.start_groups()
    for i in range(2 * AG_PARTS):
        for j, sign, far, near in ways:
            rows = (far + near)[i]
            with scope("wait_ag2"):
                ag_wait(ag_index(1, j, i), at(-2 * sign), rows)
            if i < AG_PARTS:
                ag_copy(at(-2 * sign), rows, 3, row(2 * sign)).start()
            ag_copy(at(-2 * sign), rows, 1 + j, row(sign)).start()
    for offset in (1, -1, 2, -2):
        add_grad(offset)
    with scope("wait_groups_fwd"):
        fwd.wait_groups()
    fwd.start_planes()
    for j, sign, far, near in ways:
        with scope("wait_ag3"):
            ag_wait(1 + j, at(-3 * sign))
        add_grad(-3 * sign)
    with scope("wait_ag4"):
        ag_wait(3, at(4))
    add_grad(4)
    for h in range(NH):
        bwd.put(h, tn(qrise_s[:, heads[h]], grad_s[:, heads[h]].astype(BF16)))
    bwd.start_pieces()
    with scope("wait_planes_fwd"):
        fwd.wait_planes()
    fwd.start_back()

    for h in range(NH):
        g_h = grad_s[:, heads[h]].astype(BF16)
        q_h, k_h, v_h = q_ref[:, heads[h]], k_ref[:, heads[h]], v_ref[:, heads[h]]
        pmat = (nt(g_h, v_h) * masks[h]).astype(BF16)
        qg_s[:, heads[h]] = nn(pmat, k_h)
        kg_s[:, heads[h]] = tn(pmat, q_h)
        vg_s[:, heads[h]] = tn(attn_s[h], g_h)
        vfall_s[:, heads[h]] = (fall_s[h] * v_ref[:, heads[h]].astype(F32)).astype(BF16)

    with scope("wait_pieces_bwd"):
        bwd.wait_pieces()
    bwd.start_groups()

    with scope("wait_back_fwd"):
        fwd.wait_back()
    for h in range(NH):
        out_s[:, heads[h]] += nn(qrise_s[:, heads[h]], fwd.brecv[heads[h], :])
    attn_out = out_s[...].astype(BF16)

    def part(offset):
        return nn(attn_out, w_cols(lax.rem(y + NY + offset, NY)))

    def rs_copy(slot, rows, i, where):
        return pltpu.make_async_remote_copy(rs_send.at[slot, rows], rs_recv.at[slot, rows], rs_sem.at[0], rs_sem.at[i],
                                            device_id=where, device_id_type=MESH)

    ways = ways_of(RS_PARTS)

    def rs_index(left, j, i):
        return 2 + ((left - 2) * 2 + j) * 2 * RS_PARTS + i

    def rs_slot(left, j):
        return 0 if left == 4 else 7 - 2 * left + j

    def rs_wait(slot, rows, i):
        with scope("wait_rs%d" % slot):
            rs_copy(slot, rows, i, row(1)).wait_recv()
        return rs_recv[slot, rows].astype(F32)

    def rs_on(left, i, parts):
        for j, sign, far, near in ways:
            rows, to, came = (near + far)[i], rs_slot(left, j), rs_slot(left + 1, j)
            total = parts[j][rows] + rs_wait(came, rows, rs_index(left + 1, j, i))
            if left == 2 and i >= RS_PARTS:
                total = total + rs_wait(0, rows, rs_index(4, j, i))
            rs_send[to, rows] = total.astype(BF16)
            rs_copy(to, rows, 1 if left == 1 else rs_index(left, j, i), row(sign)).start()

    rs_send[0] = part(4).astype(BF16)
    for i in range(RS_PARTS):
        for j, sign, far, near in ways:
            rs_copy(0, far[i], rs_index(4, j, RS_PARTS + i), row(2 * sign)).start()
    for j, sign, far, near in ways:
        rs_send[1 + j] = part(3 * sign).astype(BF16)
        for i in range(RS_PARTS):
            rs_copy(1 + j, far[i], rs_index(3, j, RS_PARTS + i), row(sign)).start()
    two = [part(2 * sign) for _, sign, _, _ in ways]
    for i in range(RS_PARTS):
        for j, sign, far, near in ways:
            rs_copy(1 + j, near[i], rs_index(3, j, i), row(sign)).start()
    one = [part(sign) for _, sign, _, _ in ways]
    own = part(0)

    with scope("wait_groups_bwd"):
        bwd.wait_groups()
    bwd.start_planes()

    for i in range(RS_PARTS):
        rs_on(2, RS_PARTS + i, two)
    for i in range(RS_PARTS):
        rs_on(2, i, two)
    with scope("wait_planes_bwd"):
        bwd.wait_planes()
    bwd.start_back()
    for i in range(RS_PARTS):
        rs_on(1, RS_PARTS + i, one)
    for i in range(RS_PARTS):
        rs_on(1, i, one)

    for h in range(NH):
        g_rise = (rise_s[h] * grad_s[:, heads[h]].astype(BF16).astype(F32)).astype(BF16)
        qg_ref[:, heads[h]] = (qg_s[:, heads[h]] + nt(g_rise, fwd.brecv[heads[h], :])).astype(BF16)

    with scope("wait_back_bwd"):
        bwd.wait_back()
    for h in range(NH):
        carry = bwd.brecv[heads[h], :]
        kg_ref[:, heads[h]] = (kg_s[:, heads[h]] + nt(vfall_s[:, heads[h]], carry)).astype(BF16)
        vg_ref[:, heads[h]] = (vg_s[:, heads[h]] + nn(kfall_s[:, heads[h]], carry)).astype(BF16)

    with scope("wait_rs1"):
        pltpu.make_async_remote_copy(rs_send.at[5:7], rs_recv.at[5:7], rs_sem.at[0], rs_sem.at[1],
                                     device_id=row(1), device_id_type=MESH).wait_recv()
    total = own
    for slot in (5, 6):
        total = total + rs_recv[slot].astype(F32)
    mixed_ref[...] = total.astype(BF16)

    with scope("wait_sends"):
        fwd.finish()
        bwd.finish()
        pltpu.make_async_remote_copy(ag.at[0:7], ag.at[0:7], ag_sem.at[0], ag_sem.at[1],
                                     device_id=row(1), device_id_type=MESH).wait_send()
        pltpu.make_async_remote_copy(rs_send, rs_recv, rs_sem.at[0], rs_sem.at[1],
                                     device_id=row(1), device_id_type=MESH).wait_send()


def store(*refs):
    sources, targets, sem = refs[:4], refs[4:8], refs[8]
    copies = [pltpu.make_async_copy(src, dst, sem.at[i]) for i, (src, dst) in enumerate(zip(sources, targets))]
    for copy in copies:
        copy.start()
    for copy in copies:
        copy.wait()


def local(queries, keys, values, decay_codes, out_weight, out_grad):
    vmem = pl.BlockSpec(memory_space=pltpu.VMEM)
    wide = NH * HW
    placed = [
        pltpu.with_memory_space_constraint(array, pltpu.HBM)
        for array in (queries, keys, values, decay_codes.T, out_weight, out_grad)
    ]
    results = pl.pallas_call(
        kernel,
        out_shape=(
            pltpu.VMEM((TOK, COLS), BF16),
            pltpu.VMEM((TOK, wide), BF16),
            pltpu.VMEM((TOK, wide), BF16),
            pltpu.VMEM((TOK, wide), BF16),
        ),
        in_specs=[pl.BlockSpec(memory_space=pltpu.HBM)] * 6,
        out_specs=(vmem,) * 4,
        scratch_shapes=STATE_BUFFERS + LOG_BUFFERS + STATE_BUFFERS + [
            pltpu.VMEM((TOK, wide), BF16),
            pltpu.VMEM((TOK, wide), BF16),
            pltpu.VMEM((TOK, wide), BF16),
            pltpu.VMEM((NH, TOK), jnp.int32),
            pltpu.VMEM(out_weight.shape, BF16),
            pltpu.VMEM((TOK, COLS), BF16),
            pltpu.SemaphoreType.DMA((6,)),
            pltpu.VMEM((NY, TOK, COLS), BF16),
            pltpu.SemaphoreType.DMA((4 + 8 * AG_PARTS,)),
            pltpu.VMEM((7, TOK, COLS), BF16),
            pltpu.VMEM((7, TOK, COLS), BF16),
            pltpu.SemaphoreType.DMA((2 + 12 * RS_PARTS,)),
            pltpu.VMEM((NH, TOK, TOK), BF16),
            pltpu.VMEM((TOK, wide), BF16),
            pltpu.VMEM((TOK, wide), BF16),
            pltpu.VMEM((TOK, wide), F32),
            pltpu.VMEM((TOK, wide), F32),
            pltpu.VMEM((TOK, wide), F32),
            pltpu.VMEM((TOK, wide), F32),
            pltpu.VMEM((TOK, wide), F32),
            pltpu.VMEM((NH, TOK, HW), F32),
            pltpu.VMEM((NH, TOK, HW), F32),
            pltpu.VMEM((TOK, wide), BF16),
        ],
        name="linear_attention",
        compiler_params=pltpu.CompilerParams(
            collective_id=0, has_side_effects=True, vmem_limit_bytes=40 * 1024 * 1024
        ),
    )(*placed)
    return pl.pallas_call(
        store,
        out_shape=tuple(jax.ShapeDtypeStruct(array.shape, array.dtype) for array in results),
        in_specs=[vmem] * 4,
        out_specs=tuple([pl.BlockSpec(memory_space=pltpu.HBM)] * 4),
        scratch_shapes=[pltpu.SemaphoreType.DMA((4,))],
        name="store",
    )(*[pltpu.with_memory_space_constraint(array, pltpu.VMEM) for array in results])


def solution(mesh):
    placed = (
        P("seq", "head"),
        P("seq", "head"),
        P("seq", "head"),
        P("seq", "head"),
        P("head", None),
        P("seq", "head"),
    )
    return jax.shard_map(
        local,
        mesh=mesh,
        in_specs=placed,
        out_specs=(P("seq", "head"), P("seq", "head"), P("seq", "head"), P("seq", "head")),
        check_vma=False,
    )
```
